32 devices in a mesh: unit: 8 (over y, x, core), tm: 4 (over z).
Axes of the slice: x: 2, y: 2, z: 4, core: 2. Of those that a mesh axis runs over, the one named last changes fastest.
Arguments:
- spikes: int32 [2048, 8192], P('tm', 'unit'), may hold values from 0 to 2
- stimulus: bfloat16 [2048, 64], P('tm'), may hold values from -6 to 6
- bias: float32 [8192], P('unit'), may hold values from -1.5 to 0
- hist_weight: float32 [10, 8192], P(None, 'unit'), may hold values from -0.9 to 0.9
- stim_filter: bfloat16 [8192, 64], P('unit'), may hold values from -0.5 to 0.5
- coupling_mix: float32 [10], replicated, may hold values from -3 to 3
- coupling_target: int32 [64, 4], P('unit'), may hold values from 0 to 63, as said below
- coupling_weight: bfloat16 [64, 4, 128, 128], P('unit'), may hold values from -0.059814453 to 0.059814453
Outputs:
- grad_bias: float32 [8192], P('unit')
- grad_hist: float32 [10, 8192], P(None, 'unit')
- grad_stim: float32 [8192, 64], P(('unit', 'tm'))
- grad_coupling: float32 [64, 4, 128, 128], P('unit', None, 'tm')
The draws below stay inside these ranges and needn't reach their ends.
Inputs may be any that keep to these rules, and one draw needn't show every extreme that they name: `coupling_target`: the 4 entries of a row are distinct. Among the rows of one device (8 aligned rows), the targets owned by any one device (tiles k * 8 to k * 8 + 7) are at most 2 distinct tiles, and every owner that is named gets exactly 2.
All inputs are finite; a program needn't handle non-finite values.
Results may differ from the reference program's by a relative error of at most 0.0041.
Values may be sent and summed in bfloat16 or wider, within the bound.
No kernel may reach another device: no remote copies, remote signals or barrier semaphores. Data moves between devices by JAX's collectives and lax.ppermute only.
A program may use at most 256 MiB of HBM per device.

```python
import math
import jax
import jax.numpy as jnp
from jax import lax

UNITS_DEV = 1024
TILE = 128
FAN = 4
CAP = 2
NB = 10
LAG = 128
STIM = 64
UNITS = 8192
TIME = 2048
TILES = 64
N_UNIT = 8


def draw_coupling_target(key, part):
    per_dev = UNITS_DEV // TILE
    picks = FAN // CAP
    first_key, second_key, third_key = jax.random.split(key, 3)
    favour = jax.random.randint(first_key, (N_UNIT,), 0, 1 << 16)
    noise = jax.random.randint(second_key, (N_UNIT, per_dev, N_UNIT), 0, 1 << 16)
    owner_score = (noise + favour[None, None, :]) * N_UNIT + jnp.arange(N_UNIT, dtype=jnp.int32)[None, None, :]
    owners = lax.top_k(owner_score, picks)[1].astype(jnp.int32)
    pair_noise = jax.random.randint(third_key, (N_UNIT, N_UNIT, per_dev), 0, 1 << 16)
    pair_score = pair_noise * per_dev + jnp.arange(per_dev, dtype=jnp.int32)[None, None, :]
    pairs = lax.top_k(pair_score, CAP)[1].astype(jnp.int32)
    source_dev = jnp.arange(N_UNIT, dtype=jnp.int32)[:, None, None]
    chosen = pairs[source_dev, owners]
    targets = owners[:, :, :, None] * per_dev + chosen
    return targets.reshape(N_UNIT * per_dev, FAN).astype(jnp.int32)


def plant(entries, stream_key, low, high):
    longest = entries.shape.index(max(entries.shape))
    spots = []
    for shift in (0, 1):
        where = [jax.random.randint(jax.random.fold_in(stream_key, axis), (), 0, length) for axis, length in enumerate(entries.shape)]
        where[longest] = (where[longest] + shift) % entries.shape[longest]
        spots.append(tuple(where))
    return entries.at[spots[0]].set(low).at[spots[1]].set(high)


def shard_levels(rng, extent, shards, least, largest):
    gain, own = 1.0, jax.random.fold_in(rng, 6)
    for axis_at, blocks in shards:
        heights = jnp.exp(jax.random.uniform(jax.random.fold_in(own, axis_at), (blocks,), jnp.float32, least / len(shards), largest / len(shards)))
        gain = gain * jnp.repeat(heights, extent[axis_at] // blocks).reshape([-1 if axis == axis_at else 1 for axis in range(len(extent))])
    return gain


def normal_values(key, extent, deviation, reach, cuts=(), kind=jnp.bfloat16):
    level = shard_levels(key, extent, cuts, -0.22, 0.18) if cuts else 1.0
    drawn = jax.random.normal(key, extent, jnp.float32) * deviation * level
    return jnp.minimum(jnp.maximum(drawn, -reach), reach).astype(kind)


def setup_inputs(seed: int = 0) -> dict:
    seeds = jax.random.split(jax.random.key(seed), 9)
    return {
        "spikes": plant(jax.random.randint(seeds[0], (TIME, UNITS), 0, 3), jax.random.fold_in(seeds[0], 1), 0, 2).astype(jnp.int32),
        "stimulus": normal_values(seeds[1], (TIME, STIM), 1.0, 6.0, ((0, 4),)),
        "bias": jnp.clip(-1.5 + 1.5 * jax.random.uniform(seeds[2], (UNITS,), jnp.float32) ** shard_levels(seeds[2], (UNITS,), ((0, 8),), -0.2, 0.2), -1.5, 0.0),
        "hist_weight": normal_values(seeds[3], (NB, UNITS), 0.15, 0.9, ((1, 8),), jnp.float32),
        "stim_filter": normal_values(seeds[4], (UNITS, STIM), 0.08, 0.5, ((0, 8),)),
        "coupling_mix": normal_values(seeds[5], (NB,), 0.5, 3.0, (), jnp.float32),
        "coupling_target": draw_coupling_target(jax.random.fold_in(seeds[8], 71), 0),
        "coupling_weight": normal_values(seeds[7], (TILES, FAN, TILE, TILE), 0.01, 0.059814453, ((0, 8),)),
    }


def raised_cosine(count, lag):
    low = math.log(2.0)
    high = math.log(lag + 1.0)
    spacing = (high - low) / (count - 1)
    stretched = jnp.log(jnp.arange(1, lag + 1).astype(jnp.float32) + 1.0)
    centers = low + spacing * jnp.arange(count).astype(jnp.float32)
    phases = jnp.clip((stretched[None, :] - centers[:, None]) * (math.pi / (2.0 * spacing)), -math.pi, math.pi)
    shapes = 0.5 * (1.0 + jnp.cos(phases))
    return (shapes / jnp.sum(shapes, axis=1, keepdims=True)).astype(jnp.bfloat16)


def filtered(counts, flipped):
    signal = counts.astype(jnp.float32).transpose(1, 0)[:, None, :]
    result = lax.conv_general_dilated(signal, flipped, (1,), [(LAG, 0)], dimension_numbers=("NCH", "OIH", "NCH"), precision=lax.Precision.HIGHEST)
    return result.transpose(1, 2, 0)


def reference(spikes, stimulus, bias, hist_weight, stim_filter, coupling_mix, coupling_target, coupling_weight):
    time_len = spikes.shape[0]
    basis = raised_cosine(NB, LAG)
    kernel = jnp.concatenate([jnp.zeros((NB, 1), jnp.float32), basis.astype(jnp.float32)], axis=1)
    flipped = kernel[:, ::-1][:, None, :]
    tiles = spikes.reshape(time_len, TILES, TILE).transpose(1, 0, 2)

    def first_pass(tile_counts):
        history = filtered(tile_counts, flipped)
        return jnp.sum(coupling_mix[:, None, None] * history, axis=0).astype(jnp.bfloat16)

    mixed = lax.map(first_pass, tiles)
    per_dev = UNITS_DEV // TILE
    mixed_dev = mixed.reshape(N_UNIT, per_dev, time_len, TILE)
    target_dev = coupling_target.reshape(N_UNIT, per_dev, FAN)
    weight_dev = coupling_weight.reshape(N_UNIT, per_dev, FAN, TILE, TILE)

    def add_device(total, pieces):
        mixed_here, target_here, weight_here = pieces
        products = jnp.einsum("stk,sfkn->sftn", mixed_here.astype(jnp.float32), weight_here.astype(jnp.float32))
        partial_sum = jnp.zeros((TILES, time_len, TILE), jnp.float32).at[target_here.reshape(-1)].add(products.reshape(-1, time_len, TILE))
        rounded = lax.optimization_barrier(partial_sum.astype(jnp.bfloat16)).astype(jnp.float32)
        return total + rounded, None

    coupling, _ = lax.scan(add_device, jnp.zeros((TILES, time_len, TILE), jnp.float32), (mixed_dev, target_dev, weight_dev))
    filter_tiles = stim_filter.reshape(TILES, TILE, STIM)
    bias_tiles = bias.reshape(TILES, TILE)
    weight_tiles = hist_weight.reshape(NB, TILES, TILE).transpose(1, 0, 2)
    stim_float = stimulus.astype(jnp.float32)

    def second_pass(pieces):
        tile_counts, filter_tile, bias_tile, weight_tile, coupling_tile = pieces
        history = filtered(tile_counts, flipped)
        drive = jnp.einsum("tc,uc->tu", stim_float, filter_tile.astype(jnp.float32))
        logit = bias_tile[None, :] + drive + jnp.sum(history * weight_tile[:, None, :], axis=0) + coupling_tile
        resid = tile_counts.astype(jnp.float32) - jnp.exp(logit)
        resid_bf = resid.astype(jnp.bfloat16)
        grad_b = jnp.sum(resid, axis=0) / time_len
        grad_h = jnp.sum(history * resid[None, :, :], axis=1) / time_len
        grad_s = jnp.einsum("tu,tc->uc", resid_bf.astype(jnp.float32), stim_float) / time_len
        return grad_b, grad_h, grad_s, resid_bf

    grad_b, grad_h, grad_s, resid_tiles = lax.map(second_pass, (tiles, filter_tiles, bias_tiles, weight_tiles, coupling))

    def grad_tile(pieces):
        mixed_tile, target_row = pieces
        chosen = resid_tiles[target_row]
        return jnp.einsum("tk,ftn->fkn", mixed_tile.astype(jnp.float32), chosen.astype(jnp.float32)) / time_len

    grad_coupling = lax.map(grad_tile, (mixed, coupling_target))
    grad_bias = grad_b.reshape(UNITS)
    grad_hist = grad_h.transpose(1, 0, 2).reshape(NB, UNITS)
    grad_stim = grad_s.reshape(UNITS, STIM)
    return grad_bias, grad_hist, grad_stim, grad_coupling
```

```python
import functools
import math

import jax
import jax.numpy as jnp
import numpy as np
from jax import lax
from jax.experimental import pallas as pl
from jax.experimental.pallas import tpu as pltpu
from jax.sharding import PartitionSpec as P

TILE = 128
FAN = 4
CAP = 2
NB = 10
LAG = 128
HALVES = (64, 64)
BF = jnp.bfloat16
F32 = jnp.float32
SMEM = pltpu.SMEM


def raised_cosine(count, lag):
    low = math.log(2.0)
    high = math.log(lag + 1.0)
    spacing = (high - low) / (count - 1)
    stretched = np.log(np.arange(1, lag + 1).astype(np.float64) + 1.0)
    centers = low + spacing * np.arange(count).astype(np.float64)
    phases = np.clip(
        (stretched[None, :] - centers[:, None]) * (math.pi / (2.0 * spacing)), -math.pi, math.pi
    )
    shapes = 0.5 * (1.0 + np.cos(phases))
    return (shapes / np.sum(shapes, axis=1, keepdims=True)).astype(np.float32).astype(BF)


def toeplitz():
    basis = raised_cosine(NB, LAG)
    lag = LAG + np.arange(LAG)[None, :] - np.arange(2 * LAG)[:, None]
    inside = (lag >= 1) & (lag <= LAG)
    blocks = np.where(inside[None], basis[:, np.clip(lag - 1, 0, LAG - 1)], np.zeros((), BF))
    return np.ascontiguousarray(blocks.transpose(1, 0, 2).reshape(2 * LAG, NB * LAG))


def contract(a, b, dims):
    return lax.dot_general(a, b, ((dims[:1], dims[1:]), ((), ())), preferred_element_type=F32)


def find_lowest(target, lowest, tiles_dev):
    for o in range(lowest.shape[0]):
        lowest[o] = 1 << 30
    for s in range(target.shape[0]):
        for f in range(FAN):
            t = target[s, f]
            o = lax.div(t, tiles_dev)
            lowest[o] = jnp.minimum(lowest[o], t)


def slot_of(target, lowest, s, f, tiles_dev):
    t = target[s, f]
    o = lax.div(t, tiles_dev)
    return o * CAP + (t != lowest[o]).astype(jnp.int32)


def mixing_filter(mix, toep, filt):
    total = jnp.zeros((2 * LAG, LAG), F32)
    for b in range(NB):
        total += mix[b] * toep[:, b * LAG : (b + 1) * LAG].astype(F32)
    high = total.astype(BF)
    filt[:, :LAG] = high
    filt[:, LAG:] = (total - high.astype(F32)).astype(BF)


def mix_window(window, filt):
    both = jnp.dot(window, filt, preferred_element_type=F32)
    return (both[:, :LAG] + both[:, LAG:]).astype(BF)


def add_partials(target, lowest, weight, mixed, total, out, tiles_dev):
    s = pl.program_id(0)
    for f in range(FAN):
        slot = slot_of(target, lowest, s, f, tiles_dev)
        total[slot] += contract(weight[0, f], mixed, (0, 0))

    @pl.when(s == pl.num_programs(0) - 1)
    def _():
        out[...] = total[...].astype(BF)


def late_kernel(target, mix, spikes, toep, weight, x_out, mixed_out, part, filt, total, lowest):
    tiles_dev = target.shape[0]

    @pl.when(pl.program_id(0) == 0)
    def _():
        find_lowest(target, lowest, tiles_dev)
        mixing_filter(mix, toep, filt)
        total[...] = jnp.zeros_like(total)

    x = spikes[...].astype(F32).T.astype(BF)
    x_out[0] = x
    filter_now = filt[...]
    blocks = [
        mix_window(x[:, k - LAG : k + LAG], filter_now) for k in range(LAG, x.shape[1], LAG)
    ]
    mixed = jnp.concatenate(blocks, axis=1)
    mixed_out[0] = mixed
    add_partials(target, lowest, weight, mixed, total, part, tiles_dev)


def early_kernel(
    target, mix, halo, x, toep, weight, halo_out, mixed_out, part, filt, total, lowest
):
    tiles_dev = target.shape[0]

    @pl.when(pl.program_id(0) == 0)
    def _():
        find_lowest(target, lowest, tiles_dev)
        mixing_filter(mix, toep, filt)
        total[...] = jnp.zeros_like(total)

    before = halo[...].astype(F32).T.astype(BF)
    halo_out[0] = before
    mixed = mix_window(jnp.concatenate([before, x[0]], axis=1), filt[...])
    mixed_out[0] = mixed
    add_partials(target, lowest, weight, mixed, total, part, tiles_dev)


def logit_kernel(x, halo, toep, hist_weight, bias, stim_filter, stimulus, out, rows):
    rows[...] = jnp.zeros_like(rows)
    rows[:NB] = hist_weight[...]
    rows[NB : NB + 1] = bias[...]
    columns = rows[...].T
    drive = contract(stim_filter[...], stimulus[...], (1, 1))
    start = drive + columns[:, NB : NB + 1]
    extended = jnp.concatenate([halo[0], x[0]], axis=1)
    for k in range(0, x.shape[2], LAG):
        history = jnp.dot(extended[:, k : k + 2 * LAG], toep[...], preferred_element_type=F32)
        total = start[:, k : k + LAG]
        for b in range(NB):
            total += columns[:, b : b + 1] * history[:, b * LAG : (b + 1) * LAG]
        out[0, :, k : k + LAG] = total


def resid_kernel(ids, late, early, logit, x, resid, send, total, rounded):
    total[...] = logit[...]
    for src in range(ids.shape[0]):
        for q in range(CAP):
            tile = ids[src, q]

            @pl.when(tile >= 0)
            def _():
                total[tile, :, :LAG] += early[src * CAP + q].astype(F32)
                total[tile, :, LAG:] += late[src * CAP + q].astype(F32)

    for j in range(logit.shape[0]):
        r = x[j].astype(F32) - jnp.exp(total[j])
        resid[j] = r
        rounded[j] = r.astype(BF)
    for dst in range(ids.shape[0]):
        for q in range(CAP):
            tile = ids[dst, q]

            @pl.when(tile >= 0)
            def _():
                send[dst * CAP + q] = rounded[tile]

            @pl.when(tile < 0)
            def _():
                send[dst * CAP + q] = jnp.zeros(send.shape[1:], BF)


def own_kernel(x, halo, toep, stimulus, resid_a, resid_b, stim_out, rows_out, rows):
    resid = jnp.concatenate([resid_a[0], resid_b[0]], axis=0)
    stim_out[...] = jnp.dot(resid.astype(BF), stimulus[...], preferred_element_type=F32)
    extended = jnp.concatenate([halo[0], x[0]], axis=1)
    totals = [jnp.zeros((TILE, LAG), F32) for _ in range(NB + 1)]
    for k in range(0, x.shape[2], LAG):
        history = jnp.dot(extended[:, k : k + 2 * LAG], toep[...], preferred_element_type=F32)
        piece = resid[:, k : k + LAG]
        for b in range(NB):
            totals[b] += piece * history[:, b * LAG : (b + 1) * LAG]
        totals[NB] += piece
    rows[...] = jnp.zeros_like(rows)
    for b in range(NB + 1):
        rows[b : b + 1] = jnp.sum(totals[b].T, axis=0, keepdims=True)
    rows_out[...] = rows[...]


def grad_kernel(target, recv, mixed_early, mixed_late, out, chosen, lowest):
    tiles_dev = target.shape[0]
    s = pl.program_id(0)

    @pl.when(s == 0)
    def _():
        find_lowest(target, lowest, tiles_dev)

    part = recv.shape[1]
    for f in range(FAN):
        chosen[f * part : (f + 1) * part] = recv[slot_of(target, lowest, s, f, tiles_dev)]
    mixed = jnp.concatenate([mixed_early[0], mixed_late[0]], axis=1)
    grads = contract(mixed, chosen[...], (1, 1)).astype(BF)
    out[...] = grads.reshape(out.shape)


def final_kernel(scale, *refs):
    parts, out = refs[:-1], refs[-1]
    sums = [jnp.sum(part[:, 0].astype(F32), axis=0) * scale for part in parts]
    for f in range(FAN):
        pieces = []
        for total in sums:
            wide = total.shape[1] // FAN
            pieces.append(total[:, f * wide : (f + 1) * wide])
        out[0, f] = jnp.concatenate(pieces, axis=1)


def call(kernel, name, **kw):
    limit = pltpu.CompilerParams(vmem_limit_bytes=40 << 20)
    return pl.pallas_call(kernel, name=name, compiler_params=limit, **kw)


def smem():
    return pl.BlockSpec(memory_space=SMEM)


def whole(shape, at=None):
    spot = at or (0,) * len(shape)
    return pl.BlockSpec(shape, lambda *_: spot)


def per_tile(shape, axis=0):
    return pl.BlockSpec(shape, lambda s: tuple(s if a == axis else 0 for a in range(len(shape))))


def struct(shape, dtype):
    return jax.ShapeDtypeStruct(shape, dtype)


def shards(
    spikes, stimulus, bias, hist_weight, stim_filter, coupling_mix, coupling_target, coupling_weight
):
    time_dev, units_dev = spikes.shape
    tiles_dev = units_dev // TILE
    unit_count = lax.axis_size("unit")
    time_count = lax.axis_size("tm")
    time_total = time_dev * time_count
    slots = unit_count * CAP
    late = time_dev - LAG
    toep = jnp.asarray(toeplitz())
    toep_spec = whole((2 * LAG, NB * LAG))

    tail = spikes[time_dev - LAG :].astype(BF)
    halo = lax.ppermute(tail, "tm", [(i, i + 1) for i in range(time_count - 1)])
    all_targets = lax.all_gather(coupling_target.reshape(-1), "unit", axis=0)

    part_scratch = lambda width: [
        pltpu.VMEM((2 * LAG, 2 * LAG), BF),
        pltpu.VMEM((slots, TILE, width), F32),
        SMEM((unit_count,), jnp.int32),
    ]
    weight_spec = per_tile((1, FAN, TILE, TILE))
    x, mixed_late, part_late = call(
        late_kernel,
        "late",
        grid=(tiles_dev,),
        in_specs=[smem(), smem(), per_tile((time_dev, TILE), 1), toep_spec, weight_spec],
        out_specs=[
            per_tile((1, TILE, time_dev)),
            per_tile((1, TILE, late)),
            whole((slots, TILE, late)),
        ],
        out_shape=[
            struct((tiles_dev, TILE, time_dev), BF),
            struct((tiles_dev, TILE, late), BF),
            struct((slots, TILE, late), BF),
        ],
        scratch_shapes=part_scratch(late),
    )(coupling_target, coupling_mix, spikes, toep, coupling_weight)
    got_late = lax.all_to_all(part_late, "unit", 0, 0, tiled=True)

    halo_t, mixed_early, part_early = call(
        early_kernel,
        "early",
        grid=(tiles_dev,),
        in_specs=[
            smem(),
            smem(),
            per_tile((LAG, TILE), 1),
            per_tile((1, TILE, LAG)),
            toep_spec,
            weight_spec,
        ],
        out_specs=[
            per_tile((1, TILE, LAG)),
            per_tile((1, TILE, LAG)),
            whole((slots, TILE, LAG)),
        ],
        out_shape=[
            struct((tiles_dev, TILE, LAG), BF),
            struct((tiles_dev, TILE, LAG), BF),
            struct((slots, TILE, LAG), BF),
        ],
        scratch_shapes=part_scratch(LAG),
    )(coupling_target, coupling_mix, halo, x, toep, coupling_weight)
    got_early = lax.all_to_all(part_early, "unit", 0, 0, tiled=True)

    x_spec = per_tile((1, TILE, time_dev))
    halo_spec = per_tile((1, TILE, LAG))
    stim_spec = whole(stimulus.shape)
    logit = call(
        logit_kernel,
        "logit",
        grid=(tiles_dev,),
        in_specs=[
            x_spec,
            halo_spec,
            toep_spec,
            per_tile((NB, TILE), 1),
            per_tile((1, TILE), 1),
            per_tile((TILE, stim_filter.shape[1])),
            stim_spec,
        ],
        out_specs=x_spec,
        out_shape=struct((tiles_dev, TILE, time_dev), F32),
        scratch_shapes=[pltpu.VMEM((TILE, TILE), F32)],
    )(x, halo_t, toep, hist_weight, bias.reshape(1, -1), stim_filter, stimulus)

    mine = lax.div(all_targets, tiles_dev) == lax.axis_index("unit")
    local = lax.rem(all_targets, tiles_dev)
    highest = jnp.max(jnp.where(mine, local, -1), axis=1)
    lowest = jnp.min(jnp.where(mine, local, tiles_dev), axis=1)
    ids = jnp.stack([jnp.where(highest < 0, -1, lowest), highest], axis=1)

    resids, grads = [], []
    first = 0
    for part in HALVES:
        at = (0, first // part, 0)
        resid, send = call(
            resid_kernel,
            "resid",
            grid=(1,),
            in_specs=[
                smem(),
                whole((slots, part, late), at),
                whole((slots, part, LAG), at),
                whole((tiles_dev, part, time_dev), at),
                whole((tiles_dev, part, time_dev), at),
            ],
            out_specs=[
                whole((tiles_dev, part, time_dev)),
                whole((slots, part, time_dev)),
            ],
            out_shape=[
                struct((tiles_dev, part, time_dev), F32),
                struct((slots, part, time_dev), BF),
            ],
            scratch_shapes=[
                pltpu.VMEM((tiles_dev, part, time_dev), F32),
                pltpu.VMEM((tiles_dev, part, time_dev), BF),
            ],
        )(ids, got_late, got_early, logit, x)
        resids.append(resid)
        got = lax.all_to_all(send, "unit", 0, 0, tiled=True)
        rows = TILE // time_count
        grad = call(
            grad_kernel,
            "grad",
            grid=(tiles_dev,),
            in_specs=[
                smem(),
                whole((slots, part, time_dev)),
                halo_spec,
                per_tile((1, TILE, late)),
            ],
            out_specs=per_tile((time_count, 1, rows, FAN * part), 1),
            out_shape=struct((time_count, tiles_dev, rows, FAN * part), BF),
            scratch_shapes=[
                pltpu.VMEM((FAN * part, time_dev), BF),
                SMEM((unit_count,), jnp.int32),
            ],
        )(coupling_target, got, mixed_early, mixed_late)
        grads.append(lax.all_to_all(grad, "tm", 0, 0, tiled=True))
        first += part

    stim_part, rows_part = call(
        own_kernel,
        "own",
        grid=(tiles_dev,),
        in_specs=[x_spec, halo_spec, toep_spec, stim_spec]
        + [per_tile((1, part, time_dev)) for part in HALVES],
        out_specs=[per_tile((TILE, stimulus.shape[1])), per_tile((16, TILE), 1)],
        out_shape=[
            struct((units_dev, stimulus.shape[1]), F32),
            struct((16, units_dev), F32),
        ],
        scratch_shapes=[pltpu.VMEM((16, TILE), F32)],
    )(x, halo_t, toep, stimulus, *resids)
    rows_total = lax.psum(rows_part, "tm")
    stim_got = lax.all_to_all(
        stim_part.reshape(time_count, units_dev // time_count, -1), "tm", 0, 0, tiled=True
    )
    grad_stim = jnp.sum(stim_got, axis=0) / time_total
    grad_bias = rows_total[NB] / time_total
    grad_hist = rows_total[:NB] / time_total

    rows = TILE // time_count
    grad_coupling = call(
        functools.partial(final_kernel, 1.0 / time_total),
        "final",
        grid=(tiles_dev,),
        in_specs=[per_tile((time_count, 1, rows, FAN * part), 1) for part in HALVES],
        out_specs=per_tile((1, FAN, rows, TILE)),
        out_shape=struct((tiles_dev, FAN, rows, TILE), F32),
    )(*grads)
    return (grad_bias, grad_hist, grad_stim, grad_coupling)


def solution(mesh):
    return jax.shard_map(
        shards,
        mesh=mesh,
        in_specs=(
            P("tm", "unit"),
            P("tm", None),
            P("unit"),
            P(None, "unit"),
            P("unit", None),
            P(),
            P("unit", None),
            P("unit", None, None, None),
        ),
        out_specs=(
            P("unit"),
            P(None, "unit"),
            P(("unit", "tm"), None),
            P("unit", None, "tm", None),
        ),
        check_vma=False,
    )
```

```python
import functools
import math

import jax
import jax.numpy as jnp
import numpy as np
from jax import lax
from jax.experimental import pallas as pl
from jax.experimental.pallas import tpu as pltpu
from jax.sharding import PartitionSpec as P

TILE = 128
FAN = 4
CAP = 2
NB = 10
LAG = 128
HALVES = (64, 64)
BF = jnp.bfloat16
F32 = jnp.float32
SMEM = pltpu.SMEM
VMEM_LIMIT = 40 << 20
FLOPS_A_MICRO = 1.1e9
HIST_ROWS = 16


def raised_cosine(count, lag):
    low = math.log(2.0)
    high = math.log(lag + 1.0)
    spacing = (high - low) / (count - 1)
    stretched = np.log(np.arange(1, lag + 1).astype(np.float64) + 1.0)
    centers = low + spacing * np.arange(count).astype(np.float64)
    phases = np.clip(
        (stretched[None, :] - centers[:, None]) * (math.pi / (2.0 * spacing)), -math.pi, math.pi
    )
    shapes = 0.5 * (1.0 + np.cos(phases))
    return (shapes / np.sum(shapes, axis=1, keepdims=True)).astype(np.float32).astype(BF)


def toeplitz():
    basis = raised_cosine(NB, LAG)
    lag = LAG + np.arange(LAG)[None, :] - np.arange(2 * LAG)[:, None]
    inside = (lag >= 1) & (lag <= LAG)
    blocks = np.where(inside[None], basis[:, np.clip(lag - 1, 0, LAG - 1)], np.zeros((), BF))
    return np.ascontiguousarray(blocks.transpose(1, 0, 2).reshape(2 * LAG, NB * LAG))


def contract(a, b, dims):
    return lax.dot_general(a, b, ((dims[:1], dims[1:]), ((), ())), preferred_element_type=F32)


def find_lowest(target, lowest, tiles_dev):
    for o in range(lowest.shape[0]):
        lowest[o] = 1 << 30
    for s in range(target.shape[0]):
        for f in range(FAN):
            t = target[s, f]
            o = lax.div(t, tiles_dev)
            lowest[o] = jnp.minimum(lowest[o], t)


def slot_of(target, lowest, s, f, tiles_dev):
    t = target[s, f]
    o = lax.div(t, tiles_dev)
    return o * CAP + (t != lowest[o]).astype(jnp.int32)


def mixing_filter(mix, toep, filt):
    total = jnp.zeros((2 * LAG, LAG), F32)
    for b in range(NB):
        total += mix[b] * toep[:, b * LAG : (b + 1) * LAG].astype(F32)
    high = total.astype(BF)
    filt[:, :LAG] = high
    filt[:, LAG:] = (total - high.astype(F32)).astype(BF)


def mix_window(window, filt):
    both = jnp.dot(window, filt, preferred_element_type=F32)
    return (both[:, :LAG] + both[:, LAG:]).astype(BF)


def add_partials(target, lowest, weight, mixed, total, out, tiles_dev):
    s = pl.program_id(0)
    for f in range(FAN):
        slot = slot_of(target, lowest, s, f, tiles_dev)
        total[slot] += contract(weight[0, f], mixed, (0, 0))

    @pl.when(s == pl.num_programs(0) - 1)
    def _():
        out[...] = total[...].astype(BF)


def late_kernel(target, mix, spikes, toep, weight, x_out, mixed_out, part, filt, total, lowest):
    tiles_dev = target.shape[0]

    @pl.when(pl.program_id(0) == 0)
    def _():
        find_lowest(target, lowest, tiles_dev)
        mixing_filter(mix, toep, filt)
        total[...] = jnp.zeros_like(total)

    x = spikes[...].astype(F32).T.astype(BF)
    x_out[0] = x
    filter_now = filt[...]
    blocks = [
        mix_window(x[:, k - LAG : k + LAG], filter_now) for k in range(LAG, x.shape[1], LAG)
    ]
    mixed = jnp.concatenate(blocks, axis=1)
    mixed_out[0] = mixed
    add_partials(target, lowest, weight, mixed, total, part, tiles_dev)


def early_kernel(
    target, mix, halo, x, toep, weight, kept, halo_out, mixed_out, part, named, filt, total, lowest
):
    tiles_dev = target.shape[0]
    del kept

    @pl.when(pl.program_id(0) == 0)
    def _():
        find_lowest(target, lowest, tiles_dev)
        mixing_filter(mix, toep, filt)
        total[...] = jnp.zeros_like(total)

        for o in range(lowest.shape[0]):
            for q in range(CAP):
                named[o * CAP + q] = -1
        for s in range(tiles_dev):
            for f in range(FAN):
                slot = slot_of(target, lowest, s, f, tiles_dev)
                named[slot] = lax.rem(target[s, f], tiles_dev)

    before = halo[...].astype(F32).T.astype(BF)
    halo_out[0] = before
    mixed = mix_window(jnp.concatenate([before, x[0]], axis=1), filt[...])
    mixed_out[0] = mixed
    add_partials(target, lowest, weight, mixed, total, part, tiles_dev)


def logit_kernel(x, halo, toep, hist_weight, bias, stim_filter, stimulus, out, rows):
    rows[...] = jnp.zeros_like(rows)
    rows[:NB] = hist_weight[...]
    rows[NB : NB + 1] = bias[...]
    columns = rows[...].T
    drive = contract(stim_filter[...], stimulus[...], (1, 1))
    start = drive + columns[:, NB : NB + 1]
    extended = jnp.concatenate([halo[0], x[0]], axis=1)
    for k in range(0, x.shape[2], LAG):
        history = jnp.dot(extended[:, k : k + 2 * LAG], toep[...], preferred_element_type=F32)
        total = start[:, k : k + LAG]
        for b in range(NB):
            total += columns[:, b : b + 1] * history[:, b * LAG : (b + 1) * LAG]
        out[0, :, k : k + LAG] = total


def tile_at(ids, other, q, count):
    me = lax.axis_index("unit")
    return ids[jnp.bitwise_xor(me, other) * count * CAP + me * CAP + q]


def resid_kernel(ids, got, logit, x, resid, send, total, rounded):
    total[...] = logit[...]
    count = got.shape[0] // CAP
    late = got.shape[2] - LAG
    for src in range(count):
        for q in range(CAP):
            tile = tile_at(ids, src, q, count)

            @pl.when(tile >= 0)
            def _():
                total[tile, :, LAG:] += got[src * CAP + q, :, :late].astype(F32)
                total[tile, :, :LAG] += got[src * CAP + q, :, late:].astype(F32)

    for j in range(logit.shape[0]):
        r = x[j].astype(F32) - jnp.exp(total[j])
        resid[j] = r
        rounded[j] = r.astype(BF)
    for dst in range(count):
        for q in range(CAP):
            tile = tile_at(ids, dst, q, count)

            @pl.when(tile >= 0)
            def _():
                send[dst * CAP + q] = rounded[tile]

            @pl.when(tile < 0)
            def _():
                send[dst * CAP + q] = jnp.zeros(send.shape[1:], BF)


def peer(shift, count):
    return lax.rem(lax.axis_index("tm") + shift, count)


def own_kernel(x, halo, toep, stimulus, resid_a, resid_b, *refs):
    outs, (wide, stim, sums) = refs[:-3], refs[-3:]
    s = pl.program_id(0)
    channels = stimulus.shape[1]
    rows = sums.shape[0]

    @pl.when(s == 0)
    def _():
        wide[...] = jnp.zeros_like(wide)
        wide[:, :channels] = stimulus[...]
        sums[...] = jnp.zeros_like(sums)

    resid = jnp.concatenate([resid_a[0], resid_b[0]], axis=0)
    stim[pl.ds(s * TILE, TILE)] = jnp.dot(
        resid.astype(BF), wide[...], preferred_element_type=F32
    )
    extended = jnp.concatenate([halo[0], x[0]], axis=1)
    totals = [jnp.zeros((TILE, LAG), F32) for _ in range(NB + 1)]
    for k in range(0, x.shape[2], LAG):
        history = jnp.dot(extended[:, k : k + 2 * LAG], toep[...], preferred_element_type=F32)
        piece = resid[:, k : k + LAG]
        for b in range(NB):
            totals[b] += piece * history[:, b * LAG : (b + 1) * LAG]
        totals[NB] += piece
    lane = lax.broadcasted_iota(jnp.int32, (TILE, sums.shape[1]), 1)
    first = channels + HIST_ROWS * lax.div(s * TILE, rows)
    block = jnp.zeros((TILE, sums.shape[1]), F32)
    for b in range(NB + 1):
        column = jnp.sum(totals[b], axis=1, keepdims=True)
        block = jnp.where(lane == first + b, column, block)
    at = pl.ds(pl.multiple_of(lax.rem(s * TILE, rows), TILE), TILE)
    sums[at] += block

    @pl.when(s == pl.num_programs(0) - 1)
    def _():
        for shift, out in enumerate(outs):
            first = pl.multiple_of(peer(shift, len(outs)) * rows, TILE)
            out[...] = stim[pl.ds(first, rows)] + sums[...]


def finish_kernel(scale, *refs):
    parts, (bias_out, hist_out, stim_out) = refs[:-3], refs[-3:]
    total = parts[0][...]
    for part in parts[1:]:
        total += part[...]
    total *= scale
    channels = stim_out.shape[1]
    rows = total.shape[0]
    stim_out[...] = total[:, :channels]
    flat = total.T
    for g in range(hist_out.shape[1] // rows):
        first = channels + HIST_ROWS * g
        at = slice(g * rows, (g + 1) * rows)
        hist_out[:, at] = flat[first : first + NB]
        bias_out[:, at] = flat[first + NB : first + NB + 1]


def grad_kernel(target, recv, mixed_early, mixed_late, *refs):
    outs, (chosen, grads, lowest) = refs[:-3], refs[-3:]
    tiles_dev = target.shape[0]
    s = pl.program_id(0)

    @pl.when(s == 0)
    def _():
        find_lowest(target, lowest, tiles_dev)

    part = recv.shape[1]
    for f in range(FAN):
        chosen[f * part : (f + 1) * part] = recv[slot_of(target, lowest, s, f, tiles_dev)]
    mixed = jnp.concatenate([mixed_early[0], mixed_late[0]], axis=1)
    grads[...] = contract(mixed, chosen[...], (1, 1))
    rows = TILE // len(outs)
    for shift, out in enumerate(outs):
        first = pl.multiple_of(peer(shift, len(outs)) * rows, rows)
        out[0] = grads[pl.ds(first, rows)].astype(out.dtype)


def final_kernel(scale, halves, *refs):
    parts, out = refs[:-1], refs[-1]
    count = len(parts) // halves
    sums = []
    for half in range(halves):
        mine = parts[half * count : (half + 1) * count]
        total = mine[0][0].astype(F32)
        for part in mine[1:]:
            total += part[0].astype(F32)
        sums.append(total * scale)
    for f in range(FAN):
        pieces = []
        for total in sums:
            wide = total.shape[1] // FAN
            pieces.append(total[:, f * wide : (f + 1) * wide])
        out[0, f] = jnp.concatenate(pieces, axis=1)


def to_peers(pieces):
    count = len(pieces)
    got = [pieces[0]]
    for shift in range(1, count):
        pairs = [(i, (i + shift) % count) for i in range(count)]
        got.append(lax.ppermute(pieces[shift], "tm", pairs))
    return got


def gathered(value, axis):
    step = 1
    while step < lax.axis_size(axis):
        pairs = [(i, i ^ step) for i in range(lax.axis_size(axis))]
        value = jnp.concatenate([value, lax.ppermute(value, axis, pairs)])
        step *= 2
    return value


def call(kernel, name, micros, **kw):
    limit = pltpu.CompilerParams(vmem_limit_bytes=VMEM_LIMIT)
    cost = pl.CostEstimate(
        flops=int(micros * FLOPS_A_MICRO), bytes_accessed=1 << 20, transcendentals=0
    )
    return pl.pallas_call(kernel, name=name, compiler_params=limit, cost_estimate=cost, **kw)


def smem():
    return pl.BlockSpec(memory_space=SMEM)


def whole(shape, at=None):
    spot = at or (0,) * len(shape)
    return pl.BlockSpec(shape, lambda *_: spot)


def per_tile(shape, axis=0):
    return pl.BlockSpec(shape, lambda s: tuple(s if a == axis else 0 for a in range(len(shape))))


def struct(shape, dtype):
    return jax.ShapeDtypeStruct(shape, dtype)


def shards(
    spikes, stimulus, bias, hist_weight, stim_filter, coupling_mix, coupling_target, coupling_weight
):
    time_dev, units_dev = spikes.shape
    tiles_dev = units_dev // TILE
    channels = stimulus.shape[1]
    unit_count = lax.axis_size("unit")
    time_count = lax.axis_size("tm")
    time_total = time_dev * time_count
    slots = unit_count * CAP
    late = time_dev - LAG
    toep = jnp.asarray(toeplitz())
    toep_spec = whole((2 * LAG, NB * LAG))

    tail = spikes[time_dev - LAG :].astype(BF)
    halo = lax.ppermute(tail, "tm", [(i, i + 1) for i in range(time_count - 1)])

    part_scratch = lambda width: [
        pltpu.VMEM((2 * LAG, 2 * LAG), BF),
        pltpu.VMEM((slots, TILE, width), F32),
        SMEM((unit_count,), jnp.int32),
    ]
    weight_spec = per_tile((1, FAN, TILE, TILE))
    x, mixed_late, part_late = call(
        late_kernel,
        "late",
        5,
        grid=(tiles_dev,),
        in_specs=[smem(), smem(), per_tile((time_dev, TILE), 1), toep_spec, weight_spec],
        out_specs=[
            per_tile((1, TILE, time_dev)),
            per_tile((1, TILE, late)),
            whole((slots, TILE, late)),
        ],
        out_shape=[
            struct((tiles_dev, TILE, time_dev), BF),
            struct((tiles_dev, TILE, late), BF),
            struct((slots, TILE, time_dev), BF),
        ],
        scratch_shapes=part_scratch(late),
    )(coupling_target, coupling_mix, spikes, toep, coupling_weight)

    halo_t, mixed_early, partials, named = call(
        early_kernel,
        "early",
        4,
        grid=(tiles_dev,),
        in_specs=[
            smem(),
            smem(),
            per_tile((LAG, TILE), 1),
            per_tile((1, TILE, LAG)),
            toep_spec,
            weight_spec,
            pl.BlockSpec(memory_space=pl.ANY),
        ],
        out_specs=[
            per_tile((1, TILE, LAG)),
            per_tile((1, TILE, LAG)),
            whole((slots, TILE, LAG), (0, 0, late // LAG)),
            smem(),
        ],
        out_shape=[
            struct((tiles_dev, TILE, LAG), BF),
            struct((tiles_dev, TILE, LAG), BF),
            struct((slots, TILE, time_dev), BF),
            struct((slots,), jnp.int32),
        ],
        scratch_shapes=part_scratch(LAG),
        input_output_aliases={6: 2},
    )(coupling_target, coupling_mix, halo, x, toep, coupling_weight, part_late)
    got_partials = lax.all_to_all(partials, "unit", 0, 0, tiled=True)
    ids = gathered(named, "unit")

    x_spec = per_tile((1, TILE, time_dev))
    halo_spec = per_tile((1, TILE, LAG))
    stim_spec = whole(stimulus.shape)
    logit = call(
        logit_kernel,
        "logit",
        5,
        grid=(tiles_dev,),
        in_specs=[
            x_spec,
            halo_spec,
            toep_spec,
            per_tile((NB, TILE), 1),
            per_tile((1, TILE), 1),
            per_tile((TILE, channels)),
            stim_spec,
        ],
        out_specs=x_spec,
        out_shape=struct((tiles_dev, TILE, time_dev), F32),
        scratch_shapes=[pltpu.VMEM((TILE, TILE), F32)],
    )(x, halo_t, toep, hist_weight, bias.reshape(1, -1), stim_filter, stimulus)

    rows = TILE // time_count
    resids, grads = [], []
    first = 0
    for part in HALVES:
        at = (0, first // part, 0)
        resid, send = call(
            resid_kernel,
            "resid",
            2,
            grid=(1,),
            in_specs=[
                smem(),
                whole((slots, part, time_dev), at),
                whole((tiles_dev, part, time_dev), at),
                whole((tiles_dev, part, time_dev), at),
            ],
            out_specs=[
                whole((tiles_dev, part, time_dev)),
                whole((slots, part, time_dev)),
            ],
            out_shape=[
                struct((tiles_dev, part, time_dev), F32),
                struct((slots, part, time_dev), BF),
            ],
            scratch_shapes=[
                pltpu.VMEM((tiles_dev, part, time_dev), F32),
                pltpu.VMEM((tiles_dev, part, time_dev), BF),
            ],
        )(ids, got_partials, logit, x)
        resids.append(resid)
        got = lax.all_to_all(send, "unit", 0, 0, tiled=True)
        pieces = call(
            grad_kernel,
            "grad",
            4,
            grid=(tiles_dev,),
            in_specs=[
                smem(),
                whole((slots, part, time_dev)),
                halo_spec,
                per_tile((1, TILE, late)),
            ],
            out_specs=[per_tile((1, rows, FAN * part))] * time_count,
            out_shape=[struct((tiles_dev, rows, FAN * part), BF)] * time_count,
            scratch_shapes=[
                pltpu.VMEM((FAN * part, time_dev), BF),
                pltpu.VMEM((TILE, FAN * part), F32),
                SMEM((unit_count,), jnp.int32),
            ],
        )(coupling_target, got, mixed_early, mixed_late)
        grads += to_peers(pieces)
        first += part

    own_rows = units_dev // time_count
    wide = -(-(channels + HIST_ROWS * time_count) // TILE) * TILE
    pieces = call(
        own_kernel,
        "own",
        6,
        grid=(tiles_dev,),
        in_specs=[x_spec, halo_spec, toep_spec, stim_spec]
        + [per_tile((1, part, time_dev)) for part in HALVES],
        out_specs=[whole((own_rows, wide))] * time_count,
        out_shape=[struct((own_rows, wide), F32)] * time_count,
        scratch_shapes=[
            pltpu.VMEM((time_dev, wide), BF),
            pltpu.VMEM((units_dev, wide), F32),
            pltpu.VMEM((own_rows, wide), F32),
        ],
    )(x, halo_t, toep, stimulus, *resids)
    grad_bias, grad_hist, grad_stim = call(
        functools.partial(finish_kernel, 1.0 / time_total),
        "finish",
        1,
        out_shape=[
            struct((1, units_dev), F32),
            struct((NB, units_dev), F32),
            struct((own_rows, channels), F32),
        ],
    )(*to_peers(pieces))

    grad_coupling = call(
        functools.partial(final_kernel, 1.0 / time_total, len(HALVES)),
        "final",
        2,
        grid=(tiles_dev,),
        in_specs=[
            per_tile((1, rows, FAN * part)) for part in HALVES for _ in range(time_count)
        ],
        out_specs=per_tile((1, FAN, rows, TILE)),
        out_shape=struct((tiles_dev, FAN, rows, TILE), F32),
    )(*grads)
    return (grad_bias.reshape(-1), grad_hist, grad_stim, grad_coupling)


def solution(mesh):
    return jax.shard_map(
        shards,
        mesh=mesh,
        in_specs=(
            P("tm", "unit"),
            P("tm", None),
            P("unit"),
            P(None, "unit"),
            P("unit", None),
            P(),
            P("unit", None),
            P("unit", None, None, None),
        ),
        out_specs=(
            P("unit"),
            P(None, "unit"),
            P(("unit", "tm"), None),
            P("unit", None, "tm", None),
        ),
        check_vma=False,
    )
```

```python
import functools
import math

import jax
import jax.numpy as jnp
import numpy as np
from jax import lax
from jax.experimental import pallas as pl
from jax.experimental.pallas import tpu as pltpu
from jax.sharding import PartitionSpec as P

TILE = 128
FAN = 4
CAP = 2
NB = 10
LAG = 128
HALVES = (64, 64)
BF = jnp.bfloat16
F32 = jnp.float32
SMEM = pltpu.SMEM
VMEM_LIMIT = 20 << 20
FLOPS_A_MICRO = 1.1e9
HIST_ROWS = 16
NAME_ROWS = 16


def raised_cosine(count, lag):
    low = math.log(2.0)
    high = math.log(lag + 1.0)
    spacing = (high - low) / (count - 1)
    stretched = np.log(np.arange(1, lag + 1).astype(np.float64) + 1.0)
    centers = low + spacing * np.arange(count).astype(np.float64)
    phases = np.clip(
        (stretched[None, :] - centers[:, None]) * (math.pi / (2.0 * spacing)), -math.pi, math.pi
    )
    shapes = 0.5 * (1.0 + np.cos(phases))
    return (shapes / np.sum(shapes, axis=1, keepdims=True)).astype(np.float32).astype(BF)


def toeplitz():
    basis = raised_cosine(NB, LAG)
    lag = LAG + np.arange(LAG)[None, :] - np.arange(2 * LAG)[:, None]
    inside = (lag >= 1) & (lag <= LAG)
    blocks = np.where(inside[None], basis[:, np.clip(lag - 1, 0, LAG - 1)], np.zeros((), BF))
    return np.ascontiguousarray(blocks.transpose(1, 0, 2).reshape(2 * LAG, NB * LAG))


def contract(a, b, dims):
    return lax.dot_general(a, b, ((dims[:1], dims[1:]), ((), ())), preferred_element_type=F32)


def find_lowest(target, lowest, tiles_dev):
    for o in range(lowest.shape[0]):
        lowest[o] = 1 << 30
    for s in range(target.shape[0]):
        for f in range(FAN):
            t = target[s, f]
            o = lax.div(t, tiles_dev)
            lowest[o] = jnp.minimum(lowest[o], t)


def slot_of(target, lowest, s, f, tiles_dev):
    t = target[s, f]
    o = lax.div(t, tiles_dev)
    return o * CAP + (t != lowest[o]).astype(jnp.int32)


def mixing_filter(mix, toep, filt):
    total = jnp.zeros((2 * LAG, LAG), F32)
    for b in range(NB):
        total += mix[b] * toep[:, b * LAG : (b + 1) * LAG].astype(F32)
    high = total.astype(BF)
    filt[:, :LAG] = high
    filt[:, LAG:] = (total - high.astype(F32)).astype(BF)


def mix_window(window, filt):
    both = jnp.dot(window, filt, preferred_element_type=F32)
    return (both[:, :LAG] + both[:, LAG:]).astype(BF)


def add_partials(target, lowest, turned, mixed, total, tiles_dev):
    total[...] = jnp.zeros_like(total)
    for s in range(tiles_dev):
        products = jnp.dot(turned[s], mixed[s], preferred_element_type=F32)
        for f in range(FAN):
            slot = slot_of(target, lowest, s, f, tiles_dev)
            total[slot] += products[f * TILE : (f + 1) * TILE]


def late_kernel(target, mix, spikes, weight, toep, *refs):
    x, mixed, part, tail, filt, turned = refs[:6]
    counts, weights, bases, total, lowest, highest, sems = refs[6:]
    tiles_dev = target.shape[0]
    blocks = x.shape[2] // LAG
    pulls = [
        pltpu.make_async_copy(toep, bases, sems.at[0]),
        pltpu.make_async_copy(weight, weights, sems.at[1]),
    ]
    for k in range(blocks):
        at = pl.ds(k * LAG, LAG)
        pulls.append(pltpu.make_async_copy(spikes.at[at], counts.at[at], sems.at[2 + k]))
    for pull in pulls:
        pull.start()

    find_lowest(target, lowest, tiles_dev)
    for o in range(highest.shape[0]):
        highest[o] = -1
    for s in range(tiles_dev):
        for f in range(FAN):
            t = target[s, f]
            o = lax.div(t, tiles_dev)
            highest[o] = jnp.maximum(highest[o], lax.rem(t, tiles_dev))

    pulls[0].wait()
    mixing_filter(mix, bases, filt)
    before = None
    for k in range(blocks):
        pulls[2 + k].wait()
        now = counts[k * LAG : (k + 1) * LAG].astype(F32).T.astype(BF)
        x[:, :, k * LAG : (k + 1) * LAG] = now.reshape(tiles_dev, TILE, LAG)
        if k:
            got = mix_window(jnp.concatenate([before, now], axis=1), filt[...])
            mixed[:, :, (k - 1) * LAG : k * LAG] = got.reshape(tiles_dev, TILE, LAG)
        before = now
    tail[...] = before.reshape(tiles_dev, TILE, LAG)

    pulls[1].wait()
    for s in range(tiles_dev):
        for f in range(FAN):
            turned[s, f * TILE : (f + 1) * TILE] = weights[s, f].astype(F32).T.astype(BF)
    add_partials(target, lowest, turned, mixed, total, tiles_dev)

    row = lax.broadcasted_iota(jnp.int32, (NAME_ROWS, part.shape[2]), 0)
    for o in range(part.shape[0]):
        high = highest[o]
        low = jnp.where(high < 0, -1, lax.rem(lowest[o], tiles_dev))
        for q in range(CAP):
            part[o, q * TILE : (q + 1) * TILE] = total[o * CAP + q].astype(BF)
        names = jnp.where(row == 0, low, jnp.where(row == 1, high, 0))
        part[o, CAP * TILE :] = names.astype(F32).astype(BF)


def early_kernel(target, halo, x, filt, turned, mixed_out, *refs):
    outs, (total, lowest) = refs[:-2], refs[-2:]
    tiles_dev = target.shape[0]
    units = x.shape[0] * TILE
    find_lowest(target, lowest, tiles_dev)
    window = jnp.concatenate(
        [halo[...].reshape(units, LAG), x[:, :, :LAG].reshape(units, LAG)], axis=1
    )
    mixed_out[...] = mix_window(window, filt[...]).reshape(mixed_out.shape)
    add_partials(target, lowest, turned, mixed_out, total, tiles_dev)
    me = lax.axis_index("unit")
    for k, out in enumerate(outs):
        for q in range(CAP):
            out[q] = total[jnp.bitwise_xor(me, k) * CAP + q].astype(BF)


def names_kernel(got, ids):
    for src in range(got.shape[0]):
        block = got[src].astype(F32)
        for q in range(CAP):
            ids[src * CAP + q] = jnp.max(block[q : q + 1]).astype(jnp.int32)


def logit_kernel(x, halo, toep, hist_weight, bias, stim_filter, stimulus, out, rows):
    rows[...] = jnp.zeros_like(rows)
    rows[:NB] = hist_weight[...]
    rows[NB : NB + 1] = bias[...]
    columns = rows[...].T
    drive = contract(stim_filter[...], stimulus[...], (1, 1))
    start = drive + columns[:, NB : NB + 1]
    extended = jnp.concatenate([halo[0], x[0]], axis=1)
    for k in range(0, x.shape[2], LAG):
        history = jnp.dot(extended[:, k : k + 2 * LAG], toep[...], preferred_element_type=F32)
        total = start[:, k : k + LAG]
        for b in range(NB):
            total += columns[:, b : b + 1] * history[:, b * LAG : (b + 1) * LAG]
        out[0, :, k : k + LAG] = total


def resid_kernel(first, ids, late, logit, x, *refs):
    early, (resid, send, total, rounded) = refs[:-4], refs[-4:]
    part = resid.shape[1]
    mine = slice(first, first + part)
    me = lax.axis_index("unit")
    total[...] = logit[:, mine]
    count = late.shape[0]
    for k in range(count):
        for q in range(CAP):
            tile = ids[k * CAP + q]

            @pl.when(tile >= 0)
            def _():
                start = q * TILE + first
                total[tile, :, LAG:] += late[k, start : start + part].astype(F32)

            other = ids[jnp.bitwise_xor(me, k) * CAP + q]

            @pl.when(other >= 0)
            def _():
                total[other, :, :LAG] += early[k][q, mine].astype(F32)

    for j in range(logit.shape[0]):
        r = x[j, mine].astype(F32) - jnp.exp(total[j])
        resid[j] = r
        rounded[j] = r.astype(BF)
    for dst in range(count):
        for q in range(CAP):
            tile = ids[dst * CAP + q]

            @pl.when(tile >= 0)
            def _():
                send[dst * CAP + q] = rounded[tile]

            @pl.when(tile < 0)
            def _():
                send[dst * CAP + q] = jnp.zeros(send.shape[1:], BF)


def peer(shift, count):
    return lax.rem(lax.axis_index("tm") + shift, count)


def own_kernel(x, halo, toep, stimulus, resid_a, resid_b, kept, *refs):
    outs, (passed, wide, stim, sums) = refs[:-4], refs[-4:]
    del kept, passed
    s = pl.program_id(0)
    channels = stimulus.shape[1]
    rows = sums.shape[0]

    @pl.when(s == 0)
    def _():
        wide[...] = jnp.zeros_like(wide)
        wide[:, :channels] = stimulus[...]
        sums[...] = jnp.zeros_like(sums)

    resid = jnp.concatenate([resid_a[0], resid_b[0]], axis=0)
    stim[pl.ds(s * TILE, TILE)] = jnp.dot(
        resid.astype(BF), wide[...], preferred_element_type=F32
    )
    extended = jnp.concatenate([halo[0], x[0]], axis=1)
    totals = [jnp.zeros((TILE, LAG), F32) for _ in range(NB + 1)]
    for k in range(0, x.shape[2], LAG):
        history = jnp.dot(extended[:, k : k + 2 * LAG], toep[...], preferred_element_type=F32)
        piece = resid[:, k : k + LAG]
        for b in range(NB):
            totals[b] += piece * history[:, b * LAG : (b + 1) * LAG]
        totals[NB] += piece
    lane = lax.broadcasted_iota(jnp.int32, (TILE, sums.shape[1]), 1)
    first = channels + HIST_ROWS * lax.div(s * TILE, rows)
    block = jnp.zeros((TILE, sums.shape[1]), F32)
    for b in range(NB + 1):
        column = jnp.sum(totals[b], axis=1, keepdims=True)
        block = jnp.where(lane == first + b, column, block)
    at = pl.ds(pl.multiple_of(lax.rem(s * TILE, rows), TILE), TILE)
    sums[at] += block

    @pl.when(s == pl.num_programs(0) - 1)
    def _():
        for shift, out in enumerate(outs):
            first = pl.multiple_of(peer(shift, len(outs)) * rows, TILE)
            out[...] = stim[pl.ds(first, rows)] + sums[...]


def finish_kernel(scale, *refs):
    parts, (bias_out, hist_out, stim_out) = refs[:-3], refs[-3:]
    total = parts[0][...]
    for part in parts[1:]:
        total += part[...]
    total *= scale
    channels = stim_out.shape[1]
    rows = total.shape[0]
    stim_out[...] = total[:, :channels]
    flat = total.T
    for g in range(hist_out.shape[1] // rows):
        first = channels + HIST_ROWS * g
        at = slice(g * rows, (g + 1) * rows)
        hist_out[:, at] = flat[first : first + NB]
        bias_out[:, at] = flat[first + NB : first + NB + 1]


def grad_kernel(target, recv, mixed_early, mixed_late, *refs):
    outs, (chosen, grads, lowest) = refs[:-3], refs[-3:]
    tiles_dev = target.shape[0]
    find_lowest(target, lowest, tiles_dev)
    part = recv.shape[1]
    rows = TILE // len(outs)
    for s in range(tiles_dev):
        for f in range(FAN):
            slot = slot_of(target, lowest, s, f, tiles_dev)
            chosen[s, f * part : (f + 1) * part] = recv[slot]
        mixed = jnp.concatenate([mixed_early[s], mixed_late[s]], axis=1)
        grads[s] = contract(mixed, chosen[s], (1, 1))
    for shift, out in enumerate(outs):
        first = pl.multiple_of(peer(shift, len(outs)) * rows, rows)
        out[...] = grads[:, pl.ds(first, rows)].astype(out.dtype)


def final_kernel(scale, halves, *refs):
    parts, out = refs[:-1], refs[-1]
    count = len(parts) // halves
    sums = []
    for half in range(halves):
        mine = parts[half * count : (half + 1) * count]
        total = mine[0][...].astype(F32)
        for part in mine[1:]:
            total += part[...].astype(F32)
        sums.append(total * scale)
    for f in range(FAN):
        pieces = []
        for total in sums:
            wide = total.shape[2] // FAN
            pieces.append(total[:, :, f * wide : (f + 1) * wide])
        out[:, f] = jnp.concatenate(pieces, axis=2)


def to_peers(pieces):
    count = len(pieces)
    got = [pieces[0]]
    for shift in range(1, count):
        pairs = [(i, (i + shift) % count) for i in range(count)]
        got.append(lax.ppermute(pieces[shift], "tm", pairs))
    return got


def to_units(pieces):
    got = [pieces[0]]
    for k in range(1, len(pieces)):
        got.append(lax.ppermute(pieces[k], "unit", [(i, i ^ k) for i in range(len(pieces))]))
    return got


def call(kernel, name, micros, **kw):
    limit = pltpu.CompilerParams(vmem_limit_bytes=VMEM_LIMIT)
    cost = pl.CostEstimate(
        flops=int(micros * FLOPS_A_MICRO), bytes_accessed=1 << 20, transcendentals=0
    )
    return pl.pallas_call(kernel, name=name, compiler_params=limit, cost_estimate=cost, **kw)


def vmem():
    return pl.BlockSpec(memory_space=pltpu.VMEM)


def smem():
    return pl.BlockSpec(memory_space=SMEM)


def whole(shape, at=None):
    spot = at or (0,) * len(shape)
    return pl.BlockSpec(shape, lambda *_: spot)


def per_tile(shape, axis=0):
    return pl.BlockSpec(shape, lambda s: tuple(s if a == axis else 0 for a in range(len(shape))))


def struct(shape, dtype):
    return jax.ShapeDtypeStruct(shape, dtype)


def shards(
    spikes, stimulus, bias, hist_weight, stim_filter, coupling_mix, coupling_target, coupling_weight
):
    time_dev, units_dev = spikes.shape
    tiles_dev = units_dev // TILE
    channels = stimulus.shape[1]
    unit_count = lax.axis_size("unit")
    time_count = lax.axis_size("tm")
    time_total = time_dev * time_count
    slots = unit_count * CAP
    late = time_dev - LAG
    toep = jnp.asarray(toeplitz())
    toep_spec = whole((2 * LAG, NB * LAG))

    hbm = pl.BlockSpec(memory_space=pltpu.HBM)
    find_scratch = SMEM((unit_count,), jnp.int32)
    x, mixed_late, part_late, tail, filt, turned = call(
        late_kernel,
        "late",
        5,
        in_specs=[smem(), smem(), hbm, hbm, hbm],
        out_shape=[
            struct((tiles_dev, TILE, time_dev), BF),
            struct((tiles_dev, TILE, late), BF),
            struct((unit_count, CAP * TILE + NAME_ROWS, late), BF),
            struct((tiles_dev, TILE, LAG), BF),
            struct((2 * LAG, 2 * LAG), BF),
            struct((tiles_dev, FAN * TILE, TILE), BF),
        ],
        scratch_shapes=[
            pltpu.VMEM((time_dev, units_dev), jnp.int32),
            pltpu.VMEM((tiles_dev, FAN, TILE, TILE), BF),
            pltpu.VMEM((2 * LAG, NB * LAG), BF),
            pltpu.VMEM((slots, TILE, late), F32),
            find_scratch,
            find_scratch,
            pltpu.SemaphoreType.DMA((2 + time_dev // LAG,)),
        ],
    )(coupling_target, coupling_mix, spikes, coupling_weight, toep)
    got_late = lax.all_to_all(part_late, "unit", 0, 0, tiled=True)
    halo = lax.ppermute(tail, "tm", [(i, i + 1) for i in range(time_count - 1)])

    mixed_early, *part_early = call(
        early_kernel,
        "early",
        2,
        in_specs=[smem()] + [vmem()] * 4,
        out_shape=[struct((tiles_dev, TILE, LAG), BF)]
        + [struct((CAP, TILE, LAG), BF)] * unit_count,
        scratch_shapes=[pltpu.VMEM((slots, TILE, LAG), F32), find_scratch],
    )(coupling_target, halo, x, filt, turned)
    got_early = to_units(part_early)
    ids = call(
        names_kernel,
        "names",
        1,
        grid=(1,),
        in_specs=[whole((unit_count, NAME_ROWS, LAG), (0, CAP * TILE // NAME_ROWS, 0))],
        out_specs=smem(),
        out_shape=struct((slots,), jnp.int32),
    )(got_late)

    x_spec = per_tile((1, TILE, time_dev))
    halo_spec = per_tile((1, TILE, LAG))
    stim_spec = whole(stimulus.shape)
    logit = call(
        logit_kernel,
        "logit",
        5,
        grid=(tiles_dev,),
        in_specs=[
            x_spec,
            halo_spec,
            toep_spec,
            per_tile((NB, TILE), 1),
            per_tile((1, TILE), 1),
            per_tile((TILE, channels)),
            stim_spec,
        ],
        out_specs=x_spec,
        out_shape=struct((tiles_dev, TILE, time_dev), F32),
        scratch_shapes=[pltpu.VMEM((TILE, TILE), F32)],
    )(x, halo, toep, hist_weight, bias.reshape(1, -1), stim_filter, stimulus)

    rows = TILE // time_count
    resids, sends = [], []
    for at, part in enumerate(HALVES):
        resid, send = call(
            functools.partial(resid_kernel, sum(HALVES[:at])),
            "resid",
            2,
            in_specs=[smem()] + [vmem()] * (3 + unit_count),
            out_shape=[
                struct((tiles_dev, part, time_dev), F32),
                struct((slots, part, time_dev), BF),
            ],
            scratch_shapes=[
                pltpu.VMEM((tiles_dev, part, time_dev), F32),
                pltpu.VMEM((tiles_dev, part, time_dev), BF),
            ],
        )(ids, got_late, logit, x, *got_early)
        resids.append(resid)
        sends.append(send)

    own_rows = units_dev // time_count
    wide = -(-(channels + HIST_ROWS * time_count) // TILE) * TILE
    *pieces, sends[-1] = call(
        own_kernel,
        "own",
        6,
        grid=(tiles_dev,),
        in_specs=[x_spec, halo_spec, toep_spec, stim_spec]
        + [per_tile((1, part, time_dev)) for part in HALVES]
        + [pl.BlockSpec(memory_space=pl.ANY)],
        out_specs=[whole((own_rows, wide))] * time_count + [pl.BlockSpec(memory_space=pl.ANY)],
        out_shape=[struct((own_rows, wide), F32)] * time_count
        + [struct(sends[-1].shape, BF)],
        input_output_aliases={4 + len(HALVES): time_count},
        scratch_shapes=[
            pltpu.VMEM((time_dev, wide), BF),
            pltpu.VMEM((units_dev, wide), F32),
            pltpu.VMEM((own_rows, wide), F32),
        ],
    )(x, halo, toep, stimulus, *resids, sends[-1])
    grad_bias, grad_hist, grad_stim = call(
        functools.partial(finish_kernel, 1.0 / time_total),
        "finish",
        1,
        out_shape=[
            struct((1, units_dev), F32),
            struct((NB, units_dev), F32),
            struct((own_rows, channels), F32),
        ],
    )(*to_peers(pieces))

    grads = []
    for send, part in zip(sends, HALVES, strict=True):
        got = lax.all_to_all(send, "unit", 0, 0, tiled=True)
        pieces = call(
            grad_kernel,
            "grad",
            2,
            in_specs=[smem()] + [vmem()] * 3,
            out_shape=[struct((tiles_dev, rows, FAN * part), BF)] * time_count,
            scratch_shapes=[
                pltpu.VMEM((tiles_dev, FAN * part, time_dev), BF),
                pltpu.VMEM((tiles_dev, TILE, FAN * part), F32),
                find_scratch,
            ],
        )(coupling_target, got, mixed_early, mixed_late)
        grads += to_peers(pieces)
    grad_coupling = call(
        functools.partial(final_kernel, 1.0 / time_total, len(HALVES)),
        "final",
        2,
        out_shape=struct((tiles_dev, FAN, rows, TILE), F32),
    )(*grads)
    return (grad_bias.reshape(-1), grad_hist, grad_stim, grad_coupling)


def solution(mesh):
    return jax.shard_map(
        shards,
        mesh=mesh,
        in_specs=(
            P("tm", "unit"),
            P("tm", None),
            P("unit"),
            P(None, "unit"),
            P("unit", None),
            P(),
            P("unit", None),
            P("unit", None, None, None),
        ),
        out_specs=(
            P("unit"),
            P(None, "unit"),
            P(("unit", "tm"), None),
            P("unit", None, "tm", None),
        ),
        check_vma=False,
    )
```

```python
import functools
import math

import jax
import jax.numpy as jnp
import numpy as np
from jax import lax
from jax.experimental import pallas as pl
from jax.experimental.pallas import tpu as pltpu
from jax.sharding import PartitionSpec as P

TILE = 128
FAN = 4
CAP = 2
NB = 10
LAG = 128
HALVES = (64, 64)
BF = jnp.bfloat16
F32 = jnp.float32
SMEM = pltpu.SMEM
VMEM_LIMIT = 20 << 20
FLOPS_A_MICRO = 1.1e9
HIST_ROWS = 16
NAME_ROWS = 16


def raised_cosine(count, lag):
    low = math.log(2.0)
    high = math.log(lag + 1.0)
    spacing = (high - low) / (count - 1)
    stretched = np.log(np.arange(1, lag + 1).astype(np.float64) + 1.0)
    centers = low + spacing * np.arange(count).astype(np.float64)
    phases = np.clip(
        (stretched[None, :] - centers[:, None]) * (math.pi / (2.0 * spacing)), -math.pi, math.pi
    )
    shapes = 0.5 * (1.0 + np.cos(phases))
    return (shapes / np.sum(shapes, axis=1, keepdims=True)).astype(np.float32).astype(BF)


def toeplitz():
    basis = raised_cosine(NB, LAG)
    lag = LAG + np.arange(LAG)[None, :] - np.arange(2 * LAG)[:, None]
    inside = (lag >= 1) & (lag <= LAG)
    blocks = np.where(inside[None], basis[:, np.clip(lag - 1, 0, LAG - 1)], np.zeros((), BF))
    return np.ascontiguousarray(blocks.transpose(1, 0, 2).reshape(2 * LAG, NB * LAG))


def contract(a, b, dims):
    return lax.dot_general(a, b, ((dims[:1], dims[1:]), ((), ())), preferred_element_type=F32)


def find_slots(target, slots, lowest, highest, tiles_dev):
    for o in range(lowest.shape[0]):
        lowest[o] = tiles_dev
        highest[o] = -1
    for s in range(tiles_dev):
        for f in range(FAN):
            o = lax.div(target[f, s], tiles_dev)
            tile = lax.rem(target[f, s], tiles_dev)
            lowest[o] = jnp.minimum(lowest[o], tile)
            highest[o] = jnp.maximum(highest[o], tile)
    for s in range(tiles_dev):
        for f in range(FAN):
            o = lax.div(target[f, s], tiles_dev)
            tile = lax.rem(target[f, s], tiles_dev)
            slots[s * FAN + f] = o * CAP + (tile != lowest[o]).astype(jnp.int32)


def mixing_filter(mix, toep, filt):
    total = jnp.zeros((2 * LAG, LAG), F32)
    for b in range(NB):
        total += mix[b] * toep[:, b * LAG : (b + 1) * LAG].astype(F32)
    high = total.astype(BF)
    filt[:, :LAG] = high
    filt[:, LAG:] = (total - high.astype(F32)).astype(BF)


def mix_window(window, filt):
    both = jnp.dot(window, filt, preferred_element_type=F32)
    return (both[:, :LAG] + both[:, LAG:]).astype(BF)


def add_partials(slots, turned, mixed, total):
    total[...] = jnp.zeros_like(total)
    for s in range(turned.shape[0]):
        products = jnp.dot(turned[s], mixed[s], preferred_element_type=F32)
        for f in range(FAN):
            total[slots[s * FAN + f]] += products[f * TILE : (f + 1) * TILE]


def late_kernel(target_hbm, mix_hbm, spikes, weight, toep, *refs):
    x, mixed, tail, filt, turned, slots = refs[:6]
    parts = refs[6:-9]
    target, mix, counts, weights, bases, total, lowest, highest, sems = refs[-9:]
    tiles_dev = x.shape[0]
    blocks = x.shape[2] // LAG
    pulls = [
        pltpu.make_async_copy(toep, bases, sems.at[0]),
        pltpu.make_async_copy(weight, weights, sems.at[1]),
        pltpu.make_async_copy(target_hbm, target, sems.at[2]),
        pltpu.make_async_copy(mix_hbm, mix, sems.at[3]),
    ]
    for k in range(blocks):
        at = pl.ds(k * LAG, LAG)
        pulls.append(pltpu.make_async_copy(spikes.at[at], counts.at[at], sems.at[4 + k]))
    for pull in pulls:
        pull.start()

    pulls[2].wait()
    find_slots(target, slots, lowest, highest, tiles_dev)
    pulls[3].wait()
    pulls[0].wait()
    mixing_filter(mix, bases, filt)
    before = None
    for k in range(blocks):
        pulls[4 + k].wait()
        now = counts[k * LAG : (k + 1) * LAG].astype(F32).T.astype(BF)
        x[:, :, k * LAG : (k + 1) * LAG] = now.reshape(tiles_dev, TILE, LAG)
        if k:
            got = mix_window(jnp.concatenate([before, now], axis=1), filt[...])
            mixed[:, :, (k - 1) * LAG : k * LAG] = got.reshape(tiles_dev, TILE, LAG)
        before = now
    tail[...] = before.reshape(tiles_dev, TILE, LAG)

    pulls[1].wait()
    for s in range(tiles_dev):
        for f in range(FAN):
            turned[s, f * TILE : (f + 1) * TILE] = weights[s, f].astype(F32).T.astype(BF)
    add_partials(slots, turned, mixed, total)

    row = lax.broadcasted_iota(jnp.int32, (NAME_ROWS, mixed.shape[2]), 0)
    me = lax.axis_index("unit")
    for k, part in enumerate(parts):
        o = jnp.bitwise_xor(me, k)
        high = highest[o]
        low = jnp.where(high < 0, -1, lowest[o])
        for q in range(CAP):
            part[q * TILE : (q + 1) * TILE] = total[o * CAP + q].astype(BF)
        names = jnp.where(row == 0, low, jnp.where(row == 1, high, 0))
        part[CAP * TILE :] = names.astype(F32).astype(BF)


def early_kernel(slots, halo, x, filt, turned, kept, mixed_out, *refs):
    outs, total = refs[:-2], refs[-1]
    del kept
    units = x.shape[0] * TILE
    window = jnp.concatenate(
        [halo[...].reshape(units, LAG), x[:, :, :LAG].reshape(units, LAG)], axis=1
    )
    mixed_out[...] = mix_window(window, filt[...]).reshape(mixed_out.shape)
    add_partials(slots, turned, mixed_out, total)
    me = lax.axis_index("unit")
    for k, out in enumerate(outs):
        for q in range(CAP):
            out[q] = total[jnp.bitwise_xor(me, k) * CAP + q].astype(BF)


def names_kernel(*refs):
    got, ids = refs[:-1], refs[-1]
    for k, part in enumerate(got):
        block = part[...].astype(F32)
        for q in range(CAP):
            ids[k * CAP + q] = jnp.max(block[q : q + 1]).astype(jnp.int32)


def windows(extended, count):
    return jnp.concatenate([extended[:, k * LAG : (k + 2) * LAG] for k in range(count)], axis=0)


def add_history(total, window, toep, columns):
    count = window.shape[0] // TILE
    for c in range(0, NB, 2):
        both = jnp.dot(window, toep[:, c * LAG : (c + 2) * LAG], preferred_element_type=F32)
        for b in (c, c + 1):
            weight = columns[:, b : b + 1]
            piece = both[:, (b - c) * LAG : (b - c + 1) * LAG]
            total = [
                total[k] + weight * piece[k * TILE : (k + 1) * TILE] for k in range(count)
            ]
    return total


def logit_kernel(x, toep, hist_weight, bias, stim_filter, stimulus, out, columns_out, rows):
    rows[...] = jnp.zeros_like(rows)
    rows[:NB] = hist_weight[...]
    rows[NB : NB + 1] = bias[...]
    blocks = x.shape[2] // LAG

    def one(s, _):
        units = pl.ds(pl.multiple_of(s * TILE, TILE), TILE)
        columns = rows[:, units].T
        columns_out[s] = columns
        start = contract(stim_filter[:, units], stimulus[...], (0, 0)) + columns[:, NB : NB + 1]
        total = [start[:, k * LAG : (k + 1) * LAG] for k in range(blocks)]
        window = windows(x[s], blocks - 1)
        total[1:] = add_history(total[1:], window, toep, columns)
        for k in range(blocks):
            out[s, :, k * LAG : (k + 1) * LAG] = total[k]
        return 0

    lax.fori_loop(0, x.shape[0], one, 0)


def logit_early_kernel(x, halo, toep, columns, logit, out):
    def one(s, _):
        window = jnp.concatenate([halo[s], x[s, :, :LAG]], axis=1)
        (out[s],) = add_history([logit[s, :, :LAG]], window, toep, columns[s])
        return 0

    lax.fori_loop(0, x.shape[0], one, 0)


def resid_kernel(first, ids, logit, logit_early, x, *refs):
    count = ids.shape[0] // CAP
    late, early, (resid, *sends) = refs[:count], refs[count : 2 * count], refs[2 * count : -2]
    total, rounded = refs[-2:]
    part = resid.shape[1]
    mine = slice(first, first + part)
    total[:, :, LAG:] = logit[:, mine, LAG:]
    total[:, :, :LAG] = logit_early[:, mine]
    for k in range(count):
        for q in range(CAP):
            tile = ids[k * CAP + q]

            @pl.when(tile >= 0)
            def _():
                start = q * TILE + first
                total[tile, :, LAG:] += late[k][start : start + part].astype(F32)
                total[tile, :, :LAG] += early[k][q, mine].astype(F32)

    for j in range(logit.shape[0]):
        r = x[j, mine].astype(F32) - jnp.exp(total[j])
        resid[j] = r
        rounded[j] = r.astype(BF)
    for k in range(count):
        for q in range(CAP):
            tile = ids[k * CAP + q]

            @pl.when(tile >= 0)
            def _():
                sends[k][q] = rounded[tile]

            @pl.when(tile < 0)
            def _():
                sends[k][q] = jnp.zeros(sends[k].shape[1:], BF)


def peer(shift, count):
    return lax.rem(lax.axis_index("tm") + shift, count)


def own_kernel(x, halo, toep, stimulus, resid_a, resid_b, *refs):
    outs, (wide, stim, sums) = refs[:-3], refs[-3:]
    channels = stimulus.shape[0]
    rows = sums.shape[0]
    blocks = x.shape[2] // LAG
    wide[...] = jnp.zeros_like(wide)
    wide[:channels] = stimulus[...]
    sums[...] = jnp.zeros_like(sums)
    lane = lax.broadcasted_iota(jnp.int32, (TILE, sums.shape[1]), 1)

    def one(s, _):
        resid = jnp.concatenate([resid_a[s], resid_b[s]], axis=0)
        units = pl.ds(pl.multiple_of(s * TILE, TILE), TILE)
        stim[units] = contract(resid.astype(BF), wide[...], (1, 1))
        window = windows(jnp.concatenate([halo[s], x[s]], axis=1), blocks)
        parts = [resid[:, k * LAG : (k + 1) * LAG] for k in range(blocks)]
        columns = []
        for c in range(0, NB, 2):
            both = jnp.dot(window, toep[:, c * LAG : (c + 2) * LAG], preferred_element_type=F32)
            for b in (c, c + 1):
                piece = both[:, (b - c) * LAG : (b - c + 1) * LAG]
                total = parts[0] * piece[:TILE]
                for k in range(1, blocks):
                    total += parts[k] * piece[k * TILE : (k + 1) * TILE]
                columns.append(jnp.sum(total, axis=1, keepdims=True))
        column = jnp.sum(sum(parts[1:], parts[0]), axis=1, keepdims=True)
        high = column.astype(BF).astype(F32)
        first = channels + HIST_ROWS * lax.div(s * TILE, rows)
        block = jnp.zeros((TILE, sums.shape[1]), F32)
        for b, column in enumerate(columns + [high, column - high]):
            block = jnp.where(lane == first + b, column, block)
        at = pl.ds(pl.multiple_of(lax.rem(s * TILE, rows), TILE), TILE)
        sums[at] += block
        return 0

    lax.fori_loop(0, x.shape[0], one, 0)
    for shift, out in enumerate(outs):
        first = pl.multiple_of(peer(shift, len(outs)) * rows, TILE)
        out[...] = (stim[pl.ds(first, rows)] + sums[...]).astype(out.dtype)


def finish_kernel(scale, *refs):
    parts, (bias_out, hist_out, stim_out) = refs[:-3], refs[-3:]
    total = parts[0][...]
    for part in parts[1:]:
        total += part[:, part.shape[1] - total.shape[1] :].astype(F32)
    total *= scale
    channels, rows = stim_out.shape
    flat = total.T
    stim_out[...] = flat[:channels]
    for g in range(hist_out.shape[1] // rows):
        first = channels + HIST_ROWS * g
        at = slice(g * rows, (g + 1) * rows)
        hist_out[:, at] = flat[first : first + NB]
        bias_out[:, at] = flat[first + NB : first + NB + 1] + flat[first + NB + 1 : first + NB + 2]


def grad_kernel(count, extras, slots, mixed_early, mixed_late, *refs):
    recv, extra = refs[:count], refs[count : count + extras]
    outs, (table, chosen, grads) = refs[count + extras : -3], refs[-3:]
    part = recv[0].shape[1]
    rows = TILE // len(outs)
    me = lax.axis_index("unit")
    for k in range(count):
        table[pl.ds(jnp.bitwise_xor(me, k) * CAP, CAP)] = recv[k][...]
    for s in range(mixed_early.shape[0]):
        for f in range(FAN):
            chosen[s, f * part : (f + 1) * part] = table[slots[s * FAN + f]]
        mixed = jnp.concatenate([mixed_early[s], mixed_late[s]], axis=1)
        grads[s] = contract(mixed, chosen[s], (1, 1))
    for shift, out in enumerate(outs):
        first = pl.multiple_of(peer(shift, len(outs)) * rows, rows)
        block = grads[:, pl.ds(first, rows)].astype(out.dtype)
        out[:, : FAN * part] = block.reshape(out.shape[0], FAN * part)
        if extras and shift:
            out[:, FAN * part :] = extra[shift - 1][...]


def final_kernel(scale, parts_in, *refs):
    pieces_in, out = refs[:-1], refs[-1]
    halves = len(parts_in)
    count = len(pieces_in) // halves
    sums = []
    for half, part in enumerate(parts_in):
        wide = FAN * part
        mine = pieces_in[half * count : (half + 1) * count]
        total = mine[0][:, :wide].astype(F32)
        for piece in mine[1:]:
            total += piece[:, :wide].astype(F32)
        sums.append((total * scale).reshape(out.shape[0], out.shape[2], wide))
    for f in range(FAN):
        pieces = [
            total[:, :, f * part : (f + 1) * part]
            for total, part in zip(sums, parts_in, strict=True)
        ]
        out[:, f] = jnp.concatenate(pieces, axis=2)


def to_peers(pieces):
    count = len(pieces)
    got = [pieces[0]]
    for shift in range(1, count):
        pairs = [(i, (i + shift) % count) for i in range(count)]
        got.append(lax.ppermute(pieces[shift], "tm", pairs))
    return got


def to_units(pieces):
    got = [pieces[0]]
    for k in range(1, len(pieces)):
        got.append(lax.ppermute(pieces[k], "unit", [(i, i ^ k) for i in range(len(pieces))]))
    return got


def call(kernel, name, micros, **kw):
    limit = pltpu.CompilerParams(vmem_limit_bytes=VMEM_LIMIT)
    cost = pl.CostEstimate(
        flops=int(micros * FLOPS_A_MICRO), bytes_accessed=1 << 20, transcendentals=0
    )
    return pl.pallas_call(kernel, name=name, compiler_params=limit, cost_estimate=cost, **kw)


def vmem():
    return pl.BlockSpec(memory_space=pltpu.VMEM)


def smem():
    return pl.BlockSpec(memory_space=SMEM)


def whole(shape, at=None):
    spot = at or (0,) * len(shape)
    return pl.BlockSpec(shape, lambda *_: spot)


def per_tile(shape, axis=0):
    return pl.BlockSpec(shape, lambda s: tuple(s if a == axis else 0 for a in range(len(shape))))


def struct(shape, dtype):
    return jax.ShapeDtypeStruct(shape, dtype)


def shards(
    spikes, stimulus, bias, hist_weight, stim_filter, coupling_mix, coupling_target, coupling_weight
):
    time_dev, units_dev = spikes.shape
    tiles_dev = units_dev // TILE
    channels = stimulus.shape[1]
    unit_count = lax.axis_size("unit")
    time_count = lax.axis_size("tm")
    time_total = time_dev * time_count
    slots = unit_count * CAP
    late = time_dev - LAG
    toep = jnp.asarray(toeplitz())
    toep_spec = whole((2 * LAG, NB * LAG))

    hbm = pl.BlockSpec(memory_space=pltpu.HBM)
    entry = [coupling_target.T, coupling_mix, spikes, coupling_weight, toep]
    entry = [pltpu.with_memory_space_constraint(a, pltpu.HBM) for a in entry]
    x, mixed_late, tail, filt, turned, slot_table, *part_late = call(
        late_kernel,
        "late",
        5,
        in_specs=[hbm] * len(entry),
        out_specs=[vmem()] * 5 + [smem()] + [vmem()] * unit_count,
        out_shape=[
            struct((tiles_dev, TILE, time_dev), BF),
            struct((tiles_dev, TILE, late), BF),
            struct((tiles_dev, TILE, LAG), BF),
            struct((2 * LAG, 2 * LAG), BF),
            struct((tiles_dev, FAN * TILE, TILE), BF),
            struct((tiles_dev * FAN,), jnp.int32),
        ]
        + [struct((CAP * TILE + NAME_ROWS, late), BF)] * unit_count,
        scratch_shapes=[
            SMEM((FAN, tiles_dev), jnp.int32),
            SMEM(coupling_mix.shape, F32),
            pltpu.VMEM((time_dev, units_dev), jnp.int32),
            pltpu.VMEM((tiles_dev, FAN, TILE, TILE), BF),
            pltpu.VMEM((2 * LAG, NB * LAG), BF),
            pltpu.VMEM((slots, TILE, late), F32),
            SMEM((unit_count,), jnp.int32),
            SMEM((unit_count,), jnp.int32),
            pltpu.SemaphoreType.DMA((4 + time_dev // LAG,)),
        ],
    )(*entry)
    halo = lax.ppermute(tail, "tm", [(i, i + 1) for i in range(time_count - 1)])
    got_late = to_units(part_late)

    stimulus_t = stimulus.T
    logit_shape = struct((tiles_dev, TILE, time_dev), F32)
    logit, columns = call(
        logit_kernel,
        "logit",
        4,
        in_specs=[vmem()] * 6,
        out_shape=[logit_shape, struct((tiles_dev, TILE, TILE), F32)],
        scratch_shapes=[pltpu.VMEM((TILE, units_dev), F32)],
    )(x, toep, hist_weight, bias.reshape(1, -1), stim_filter.T, stimulus_t)
    anywhere = pl.BlockSpec(memory_space=pl.ANY)
    mixed_early, *part_early, logit = call(
        early_kernel,
        "early",
        2,
        in_specs=[smem()] + [vmem()] * 4 + [anywhere],
        out_specs=[vmem()] * (1 + unit_count) + [anywhere],
        out_shape=[struct((tiles_dev, TILE, LAG), BF)]
        + [struct((CAP, TILE, LAG), BF)] * unit_count
        + [logit_shape],
        scratch_shapes=[pltpu.VMEM((slots, TILE, LAG), F32)],
        input_output_aliases={5: 1 + unit_count},
    )(slot_table, halo, x, filt, turned, logit)
    got_early = to_units(part_early)
    logit_early = call(
        logit_early_kernel,
        "logit_early",
        1,
        in_specs=[vmem()] * 5,
        out_shape=struct((tiles_dev, TILE, LAG), F32),
    )(x, halo, toep, columns, logit)
    ids = call(
        names_kernel,
        "names",
        1,
        grid=(1,),
        in_specs=[whole((NAME_ROWS, LAG), (CAP * TILE // NAME_ROWS, 0))] * unit_count,
        out_specs=smem(),
        out_shape=struct((slots,), jnp.int32),
    )(*got_late)

    rows = TILE // time_count
    resids, sends = [], []
    for at, part in enumerate(HALVES):
        resid, *send = call(
            functools.partial(resid_kernel, sum(HALVES[:at])),
            "resid",
            2,
            in_specs=[smem()] + [vmem()] * (3 + 2 * unit_count),
            out_shape=[struct((tiles_dev, part, time_dev), F32)]
            + [struct((CAP, part, time_dev), BF)] * unit_count,
            scratch_shapes=[
                pltpu.VMEM((tiles_dev, part, time_dev), F32),
                pltpu.VMEM((tiles_dev, part, time_dev), BF),
            ],
        )(ids, logit, logit_early, x, *got_late, *got_early)
        resids.append(resid)
        sends.append(send)

    own_rows = units_dev // time_count
    wide = -(-(channels + HIST_ROWS * time_count) // TILE) * TILE
    own, *extra = call(
        own_kernel,
        "own",
        4,
        in_specs=[vmem()] * 6,
        out_shape=[
            struct((own_rows, wide), F32 if shift == 0 else BF) for shift in range(time_count)
        ],
        scratch_shapes=[
            pltpu.VMEM((wide, time_dev), BF),
            pltpu.VMEM((units_dev, wide), F32),
            pltpu.VMEM((own_rows, wide), F32),
        ],
    )(x, halo, toep, stimulus_t, *resids)

    grads = []
    for send, part in zip(sends, HALVES, strict=True):
        got = to_units(send)
        extras = [] if grads else extra
        widths = [FAN * part] + [FAN * part + (wide if extras else 0)] * (time_count - 1)
        pieces = call(
            functools.partial(grad_kernel, unit_count, len(extras)),
            "grad",
            2,
            in_specs=[smem()] + [vmem()] * (2 + unit_count + len(extras)),
            out_shape=[struct((own_rows, width), BF) for width in widths],
            scratch_shapes=[
                pltpu.VMEM((slots, part, time_dev), BF),
                pltpu.VMEM((tiles_dev, FAN * part, time_dev), BF),
                pltpu.VMEM((tiles_dev, TILE, FAN * part), F32),
            ],
        )(slot_table, mixed_early, mixed_late, *got, *extras)
        grads += to_peers(pieces)
    grad_bias, grad_hist, grad_stim = call(
        functools.partial(finish_kernel, 1.0 / time_total),
        "finish",
        1,
        out_shape=[
            struct((1, units_dev), F32),
            struct((NB, units_dev), F32),
            struct((channels, own_rows), F32),
        ],
    )(own, *grads[1:time_count])
    grad_coupling = call(
        functools.partial(final_kernel, 1.0 / time_total, HALVES),
        "final",
        2,
        out_shape=struct((tiles_dev, FAN, TILE // time_count, TILE), F32),
    )(*grads)
    return (grad_bias.reshape(-1), grad_hist, grad_stim.T, grad_coupling)


def solution(mesh):
    return jax.shard_map(
        shards,
        mesh=mesh,
        in_specs=(
            P("tm", "unit"),
            P("tm", None),
            P("unit"),
            P(None, "unit"),
            P("unit", None),
            P(),
            P("unit", None),
            P("unit", None, None, None),
        ),
        out_specs=(
            P("unit"),
            P(None, "unit"),
            P(("unit", "tm"), None),
            P("unit", None, "tm", None),
        ),
        check_vma=False,
    )
```

```python
import functools
import math

import jax
import jax.numpy as jnp
import numpy as np
from jax import lax
from jax.experimental import pallas as pl
from jax.experimental.pallas import tpu as pltpu
from jax.sharding import PartitionSpec as P

TILE = 128
FAN = 4
CAP = 2
NB = 10
LAG = 128
HALVES = (64, 64)
BF = jnp.bfloat16
F32 = jnp.float32
SMEM = pltpu.SMEM
VMEM_LIMIT = 16 << 20
FLOPS_A_MICRO = 1e7
HIST_ROWS = 16
NAME_ROWS = 16


def raised_cosine(count, lag):
    low = math.log(2.0)
    high = math.log(lag + 1.0)
    spacing = (high - low) / (count - 1)
    stretched = np.log(np.arange(1, lag + 1).astype(np.float64) + 1.0)
    centers = low + spacing * np.arange(count).astype(np.float64)
    phases = np.clip(
        (stretched[None, :] - centers[:, None]) * (math.pi / (2.0 * spacing)), -math.pi, math.pi
    )
    shapes = 0.5 * (1.0 + np.cos(phases))
    return (shapes / np.sum(shapes, axis=1, keepdims=True)).astype(np.float32).astype(BF)


def toeplitz():
    basis = raised_cosine(NB, LAG)
    lag = LAG + np.arange(LAG)[None, :] - np.arange(2 * LAG)[:, None]
    inside = (lag >= 1) & (lag <= LAG)
    blocks = np.where(inside[None], basis[:, np.clip(lag - 1, 0, LAG - 1)], np.zeros((), BF))
    return np.ascontiguousarray(blocks.transpose(1, 0, 2).reshape(2 * LAG, NB * LAG))


def contract(a, b, dims):
    return lax.dot_general(a, b, ((dims[:1], dims[1:]), ((), ())), preferred_element_type=F32)


def find_slots(target, slots, lowest, highest, tiles_dev):
    for o in range(lowest.shape[0]):
        lowest[o] = tiles_dev
        highest[o] = -1
    for s in range(tiles_dev):
        for f in range(FAN):
            o = lax.div(target[f, s], tiles_dev)
            tile = lax.rem(target[f, s], tiles_dev)
            lowest[o] = jnp.minimum(lowest[o], tile)
            highest[o] = jnp.maximum(highest[o], tile)
    for s in range(tiles_dev):
        for f in range(FAN):
            o = lax.div(target[f, s], tiles_dev)
            tile = lax.rem(target[f, s], tiles_dev)
            slots[s * FAN + f] = o * CAP + (tile != lowest[o]).astype(jnp.int32)


def mixing_filter(mix, toep, filt):
    total = jnp.zeros((2 * LAG, LAG), F32)
    for b in range(NB):
        total += mix[b] * toep[:, b * LAG : (b + 1) * LAG].astype(F32)
    high = total.astype(BF)
    filt[:, :LAG] = high
    filt[:, LAG:] = (total - high.astype(F32)).astype(BF)


def mix_window(window, filt):
    both = jnp.dot(window, filt, preferred_element_type=F32)
    return (both[:, :LAG] + both[:, LAG:]).astype(BF)


def add_partials(slots, turned, mixed, total):
    total[...] = jnp.zeros_like(total)
    for s in range(turned.shape[0]):
        products = jnp.dot(turned[s], mixed[s], preferred_element_type=F32)
        for f in range(FAN):
            total[slots[s * FAN + f]] += products[f * TILE : (f + 1) * TILE]


def late_kernel(target_hbm, mix_hbm, spikes, weight, toep, *refs):
    x, mixed, filt, turned, slots = refs[:5]
    parts = refs[5:-9]
    target, mix, counts, weights, bases, total, lowest, highest, sems = refs[-9:]
    tiles_dev = x.shape[0]
    blocks = x.shape[2] // LAG
    pulls = [
        pltpu.make_async_copy(toep, bases, sems.at[0]),
        pltpu.make_async_copy(weight, weights, sems.at[1]),
        pltpu.make_async_copy(target_hbm, target, sems.at[2]),
        pltpu.make_async_copy(mix_hbm, mix, sems.at[3]),
    ]
    for k in range(blocks):
        at = pl.ds(k * LAG, LAG)
        pulls.append(pltpu.make_async_copy(spikes.at[at], counts.at[at], sems.at[4 + k]))
    for pull in pulls:
        pull.start()

    pulls[2].wait()
    find_slots(target, slots, lowest, highest, tiles_dev)
    pulls[3].wait()
    pulls[0].wait()
    mixing_filter(mix, bases, filt)
    before = None
    for k in range(blocks):
        pulls[4 + k].wait()
        now = counts[k * LAG : (k + 1) * LAG].astype(F32).T.astype(BF)
        x[:, :, k * LAG : (k + 1) * LAG] = now.reshape(tiles_dev, TILE, LAG)
        if k:
            got = mix_window(jnp.concatenate([before, now], axis=1), filt[...])
            mixed[:, :, (k - 1) * LAG : k * LAG] = got.reshape(tiles_dev, TILE, LAG)
        before = now

    pulls[1].wait()
    for s in range(tiles_dev):
        for f in range(FAN):
            turned[s, f * TILE : (f + 1) * TILE] = weights[s, f].astype(F32).T.astype(BF)
    add_partials(slots, turned, mixed, total)

    row = lax.broadcasted_iota(jnp.int32, (NAME_ROWS, LAG), 0)
    me = lax.axis_index("unit")
    for j, part in enumerate(parts):
        o = jnp.bitwise_xor(me, j)
        for k in range(1, blocks):
            for q in range(CAP):
                at = (k * CAP + q) * TILE
                block = total[o * CAP + q, :, (k - 1) * LAG : k * LAG]
                part[at : at + TILE] = block.astype(BF)
        high = highest[o]
        low = jnp.where(high < 0, -1, lowest[o])
        names = jnp.where(row == 0, low, jnp.where(row == 1, high, 0))
        part[blocks * CAP * TILE :] = names.astype(F32).astype(BF)


def early_kernel(slots, halo, x, filt, turned, *refs):
    kept = len(refs) // 2 - 1
    mixed_out, outs, total = refs[kept], refs[kept + 1 : -1], refs[-1]
    units = x.shape[0] * TILE
    now = halo[...].astype(F32).T.astype(BF)
    window = jnp.concatenate([now, x[...].reshape(units, LAG)], axis=1)
    mixed_out[...] = mix_window(window, filt[...]).reshape(mixed_out.shape)
    add_partials(slots, turned, mixed_out, total)
    me = lax.axis_index("unit")
    for k, out in enumerate(outs):
        for q in range(CAP):
            block = total[jnp.bitwise_xor(me, k) * CAP + q]
            out[q * TILE : (q + 1) * TILE] = block.astype(BF)


def names_kernel(*refs):
    got, ids = refs[:-1], refs[-1]
    for k, part in enumerate(got):
        block = part[...].astype(F32)
        for q in range(CAP):
            ids[k * CAP + q] = jnp.max(block[q : q + 1]).astype(jnp.int32)


def windows(extended, count):
    return jnp.concatenate([extended[:, k * LAG : (k + 2) * LAG] for k in range(count)], axis=0)


def logit_kernel(x, halo, toep, hist_weight, bias, stim_filter, stimulus, out, history, rows):
    rows[...] = jnp.zeros_like(rows)
    rows[:NB] = hist_weight[...]
    rows[NB : NB + 1] = bias[...]
    blocks = x.shape[2] // LAG

    def one(s, _):
        units = pl.ds(pl.multiple_of(s * TILE, TILE), TILE)
        columns = rows[:, units].T
        start = contract(stim_filter[:, units], stimulus[...], (0, 0)) + columns[:, NB : NB + 1]
        total = [start[:, k * LAG : (k + 1) * LAG] for k in range(blocks)]
        before = halo[:, units].astype(F32).T.astype(BF)
        window = windows(jnp.concatenate([before, x[s]], axis=1), blocks)
        for c in range(0, NB, 2):
            both = jnp.dot(window, toep[:, c * LAG : (c + 2) * LAG], preferred_element_type=F32)
            for b in (c, c + 1):
                weight = columns[:, b : b + 1]
                piece = both[:, (b - c) * LAG : (b - c + 1) * LAG]
                for k in range(blocks):
                    part = piece[k * TILE : (k + 1) * TILE]
                    history[s, b, :, k * LAG : (k + 1) * LAG] = part
                    total[k] += weight * part
        for k in range(blocks):
            out[s, :, k * LAG : (k + 1) * LAG] = total[k]
        return 0

    lax.fori_loop(0, x.shape[0], one, 0)


def resid_kernel(first, ids, logit, x, *refs):
    count = ids.shape[0] // CAP
    got, (resid, *sends), (total, rounded) = refs[:count], refs[count:-2], refs[-2:]
    part = resid.shape[1]
    mine = slice(first, first + part)
    total[...] = logit[:, mine]
    for j in range(count):
        for q in range(CAP):
            tile = ids[j * CAP + q]

            @pl.when(tile >= 0)
            def _():
                for k in range(x.shape[2] // LAG):
                    start = (k * CAP + q) * TILE + first
                    total[tile, :, k * LAG : (k + 1) * LAG] += got[j][start : start + part].astype(
                        F32
                    )

    for j in range(logit.shape[0]):
        r = x[j, mine].astype(F32) - jnp.exp(total[j])
        resid[j] = r
        rounded[j] = r.astype(BF)
    for k in range(count):
        for q in range(CAP):
            tile = ids[k * CAP + q]

            @pl.when(tile >= 0)
            def _():
                sends[k][q] = rounded[tile]

            @pl.when(tile < 0)
            def _():
                sends[k][q] = jnp.zeros(sends[k].shape[1:], BF)


def peer(shift, count):
    return lax.rem(lax.axis_index("tm") + shift, count)


def own_kernel(history, stimulus, resid_a, resid_b, *refs):
    outs, (wide, stim, sums) = refs[:-3], refs[-3:]
    channels = stimulus.shape[0]
    rows = sums.shape[0]
    wide[...] = jnp.zeros_like(wide)
    wide[:channels] = stimulus[...]
    sums[...] = jnp.zeros_like(sums)
    lane = lax.broadcasted_iota(jnp.int32, (TILE, sums.shape[1]), 1)

    def folded(value):
        total = value[:, :LAG]
        for k in range(LAG, value.shape[1], LAG):
            total += value[:, k : k + LAG]
        return jnp.sum(total, axis=1, keepdims=True)

    def one(s, _):
        resid = jnp.concatenate([resid_a[s], resid_b[s]], axis=0)
        units = pl.ds(pl.multiple_of(s * TILE, TILE), TILE)
        stim[units] = contract(resid.astype(BF), wide[...], (1, 1))
        columns = [folded(resid * history[s, b]) for b in range(NB)]
        column = folded(resid)
        high = column.astype(BF).astype(F32)
        first = channels + HIST_ROWS * lax.div(s * TILE, rows)
        block = jnp.zeros((TILE, sums.shape[1]), F32)
        for b, column in enumerate(columns + [high, column - high]):
            block = jnp.where(lane == first + b, column, block)
        at = pl.ds(pl.multiple_of(lax.rem(s * TILE, rows), TILE), TILE)
        sums[at] += block
        return 0

    lax.fori_loop(0, history.shape[0], one, 0)
    for shift, out in enumerate(outs):
        first = pl.multiple_of(peer(shift, len(outs)) * rows, TILE)
        out[...] = (stim[pl.ds(first, rows)] + sums[...]).astype(out.dtype)


def finish_kernel(scale, *refs):
    parts, (bias_out, hist_out, stim_out) = refs[:-3], refs[-3:]
    total = parts[0][...]
    for part in parts[1:]:
        total += part[:, part.shape[1] - total.shape[1] :].astype(F32)
    total *= scale
    channels, rows = stim_out.shape
    flat = total.T
    stim_out[...] = flat[:channels]
    for g in range(hist_out.shape[1] // rows):
        first = channels + HIST_ROWS * g
        at = slice(g * rows, (g + 1) * rows)
        hist_out[:, at] = flat[first : first + NB]
        bias_out[:, at] = flat[first + NB : first + NB + 1] + flat[first + NB + 1 : first + NB + 2]


def grad_kernel(count, extras, slots, mixed_early, mixed_late, *refs):
    recv, extra = refs[:count], refs[count : count + extras]
    outs, (table, chosen, grads) = refs[count + extras : -3], refs[-3:]
    part = recv[0].shape[1]
    rows = TILE // len(outs)
    me = lax.axis_index("unit")
    for k in range(count):
        table[pl.ds(jnp.bitwise_xor(me, k) * CAP, CAP)] = recv[k][...]
    for s in range(mixed_early.shape[0]):
        for f in range(FAN):
            chosen[s, f * part : (f + 1) * part] = table[slots[s * FAN + f]]
        mixed = jnp.concatenate([mixed_early[s], mixed_late[s]], axis=1)
        grads[s] = contract(mixed, chosen[s], (1, 1))
    for shift, out in enumerate(outs):
        first = pl.multiple_of(peer(shift, len(outs)) * rows, rows)
        block = grads[:, pl.ds(first, rows)].astype(out.dtype)
        out[:, : FAN * part] = block.reshape(out.shape[0], FAN * part)
        if extras and shift:
            out[:, FAN * part :] = extra[shift - 1][...]


def final_kernel(scale, parts_in, *refs):
    pieces_in, out = refs[:-1], refs[-1]
    halves = len(parts_in)
    count = len(pieces_in) // halves
    sums = []
    for half, part in enumerate(parts_in):
        wide = FAN * part
        mine = pieces_in[half * count : (half + 1) * count]
        total = mine[0][:, :wide].astype(F32)
        for piece in mine[1:]:
            total += piece[:, :wide].astype(F32)
        sums.append((total * scale).reshape(out.shape[0], out.shape[2], wide))
    for f in range(FAN):
        pieces = [
            total[:, :, f * part : (f + 1) * part]
            for total, part in zip(sums, parts_in, strict=True)
        ]
        out[:, f] = jnp.concatenate(pieces, axis=2)


def to_peers(pieces):
    count = len(pieces)
    got = [pieces[0]]
    for shift in range(1, count):
        pairs = [(i, (i + shift) % count) for i in range(count)]
        got.append(lax.ppermute(pieces[shift], "tm", pairs))
    return got


def to_units(pieces):
    got = [pieces[0]]
    for k in range(1, len(pieces)):
        got.append(lax.ppermute(pieces[k], "unit", [(i, i ^ k) for i in range(len(pieces))]))
    return got


def call(kernel, name, micros, **kw):
    limit = pltpu.CompilerParams(vmem_limit_bytes=VMEM_LIMIT)
    cost = pl.CostEstimate(
        flops=int(micros * FLOPS_A_MICRO), bytes_accessed=1 << 20, transcendentals=0
    )
    return pl.pallas_call(kernel, name=name, compiler_params=limit, cost_estimate=cost, **kw)


def vmem():
    return pl.BlockSpec(memory_space=pltpu.VMEM)


def smem():
    return pl.BlockSpec(memory_space=SMEM)


def whole(shape, at=None):
    spot = at or (0,) * len(shape)
    return pl.BlockSpec(shape, lambda *_: spot)


def per_tile(shape, axis=0):
    return pl.BlockSpec(shape, lambda s: tuple(s if a == axis else 0 for a in range(len(shape))))


def struct(shape, dtype):
    return jax.ShapeDtypeStruct(shape, dtype)


def far(array):
    return pltpu.with_memory_space_constraint(array, pltpu.HBM)


def shards(
    spikes, stimulus, bias, hist_weight, stim_filter, coupling_mix, coupling_target, coupling_weight
):
    time_dev, units_dev = spikes.shape
    tiles_dev = units_dev // TILE
    channels = stimulus.shape[1]
    unit_count = lax.axis_size("unit")
    time_count = lax.axis_size("tm")
    time_total = time_dev * time_count
    slots = unit_count * CAP
    late = time_dev - LAG
    toep = jnp.asarray(toeplitz())

    tail = spikes[time_dev - LAG :].astype(BF)
    halo = lax.ppermute(tail, "tm", [(i, i + 1) for i in range(time_count - 1)])

    hbm = pl.BlockSpec(memory_space=pltpu.HBM)
    entry = [coupling_target.T, coupling_mix, spikes, coupling_weight, toep]
    message = struct((CAP * time_dev + NAME_ROWS, LAG), BF)
    x, mixed_late, filt, turned, slot_table, *parts = call(
        late_kernel,
        "late",
        5,
        in_specs=[hbm] * len(entry),
        out_specs=[vmem()] * 4 + [smem()] + [vmem()] * unit_count,
        out_shape=[
            struct((tiles_dev, TILE, time_dev), BF),
            struct((tiles_dev, TILE, late), BF),
            struct((2 * LAG, 2 * LAG), BF),
            struct((tiles_dev, FAN * TILE, TILE), BF),
            struct((tiles_dev * FAN,), jnp.int32),
        ]
        + [message] * unit_count,
        scratch_shapes=[
            SMEM((FAN, tiles_dev), jnp.int32),
            SMEM(coupling_mix.shape, F32),
            pltpu.VMEM((time_dev, units_dev), jnp.int32),
            pltpu.VMEM((tiles_dev, FAN, TILE, TILE), BF),
            pltpu.VMEM((2 * LAG, NB * LAG), BF),
            pltpu.VMEM((slots, TILE, late), F32),
            SMEM((unit_count,), jnp.int32),
            SMEM((unit_count,), jnp.int32),
            pltpu.SemaphoreType.DMA((4 + time_dev // LAG,)),
        ],
    )(*[far(a) for a in entry])
    block_whole = whole((tiles_dev, TILE, LAG))
    anywhere = pl.BlockSpec(memory_space=pl.ANY)
    mixed_early, *parts = call(
        early_kernel,
        "early",
        2,
        grid=(1,),
        in_specs=[
            smem(),
            whole((LAG, units_dev)),
            block_whole,
            whole(filt.shape),
            whole(turned.shape),
        ]
        + [anywhere] * unit_count,
        out_specs=[block_whole] + [whole((CAP * TILE, LAG))] * unit_count,
        out_shape=[struct((tiles_dev, TILE, LAG), BF)] + [message] * unit_count,
        scratch_shapes=[pltpu.VMEM((slots, TILE, LAG), F32)],
        input_output_aliases={5 + k: 1 + k for k in range(unit_count)},
    )(slot_table, halo, x, filt, turned, *parts)
    got_parts = to_units(parts)
    stimulus_t = stimulus.T
    logit, history = call(
        logit_kernel,
        "logit",
        5,
        in_specs=[vmem()] * 7,
        out_shape=[
            struct((tiles_dev, TILE, time_dev), F32),
            pltpu.VMEM((tiles_dev, NB, TILE, time_dev), F32),
        ],
        scratch_shapes=[pltpu.VMEM((TILE, units_dev), F32)],
    )(x, halo, toep, hist_weight, bias.reshape(1, -1), stim_filter.T, stimulus_t)
    ids = call(
        names_kernel,
        "names",
        1,
        grid=(1,),
        in_specs=[whole((NAME_ROWS, LAG), (CAP * time_dev // NAME_ROWS, 0))] * unit_count,
        out_specs=smem(),
        out_shape=struct((slots,), jnp.int32),
    )(*got_parts)

    resids, sends = [], []
    for at, part in enumerate(HALVES):
        resid, *send = call(
            functools.partial(resid_kernel, sum(HALVES[:at])),
            "resid",
            2,
            in_specs=[smem()] + [vmem()] * (2 + unit_count),
            out_shape=[struct((tiles_dev, part, time_dev), F32)]
            + [struct((CAP, part, time_dev), BF)] * unit_count,
            scratch_shapes=[
                pltpu.VMEM((tiles_dev, part, time_dev), F32),
                pltpu.VMEM((tiles_dev, part, time_dev), BF),
            ],
        )(ids, logit, x, *got_parts)
        resids.append(resid)
        sends.append(send)

    own_rows = units_dev // time_count
    wide = -(-(channels + HIST_ROWS * time_count) // TILE) * TILE
    own, *extra = call(
        own_kernel,
        "own",
        4,
        in_specs=[vmem()] * 4,
        out_shape=[
            struct((own_rows, wide), F32 if shift == 0 else BF) for shift in range(time_count)
        ],
        scratch_shapes=[
            pltpu.VMEM((wide, time_dev), BF),
            pltpu.VMEM((units_dev, wide), F32),
            pltpu.VMEM((own_rows, wide), F32),
        ],
    )(history, stimulus_t, *resids)

    grads = []
    for send, part in zip(sends, HALVES, strict=True):
        got = to_units(send)
        extras = [] if grads else extra
        widths = [FAN * part] + [FAN * part + (wide if extras else 0)] * (time_count - 1)
        pieces = call(
            functools.partial(grad_kernel, unit_count, len(extras)),
            "grad",
            2,
            in_specs=[smem()] + [vmem()] * (2 + unit_count + len(extras)),
            out_shape=[struct((own_rows, width), BF) for width in widths],
            scratch_shapes=[
                pltpu.VMEM((slots, part, time_dev), BF),
                pltpu.VMEM((tiles_dev, FAN * part, time_dev), BF),
                pltpu.VMEM((tiles_dev, TILE, FAN * part), F32),
            ],
        )(slot_table, mixed_early, mixed_late, *got, *extras)
        grads += to_peers(pieces)
    grad_bias, grad_hist, grad_stim = call(
        functools.partial(finish_kernel, 1.0 / time_total),
        "finish",
        1,
        out_shape=[
            struct((1, units_dev), F32),
            struct((NB, units_dev), F32),
            struct((channels, own_rows), F32),
        ],
    )(own, *grads[1:time_count])
    grad_coupling = call(
        functools.partial(final_kernel, 1.0 / time_total, HALVES),
        "final",
        2,
        out_shape=struct((tiles_dev, FAN, TILE // time_count, TILE), F32),
    )(*grads)
    return (grad_bias.reshape(-1), grad_hist, grad_stim.T, grad_coupling)


def solution(mesh):
    return jax.shard_map(
        shards,
        mesh=mesh,
        in_specs=(
            P("tm", "unit"),
            P("tm", None),
            P("unit"),
            P(None, "unit"),
            P("unit", None),
            P(),
            P("unit", None),
            P("unit", None, None, None),
        ),
        out_specs=(
            P("unit"),
            P(None, "unit"),
            P(("unit", "tm"), None),
            P("unit", None, "tm", None),
        ),
        check_vma=False,
    )
```

```python
import functools
import math

import jax
import jax.numpy as jnp
import numpy as np
from jax import lax
from jax.experimental import pallas as pl
from jax.experimental.pallas import tpu as pltpu
from jax.sharding import PartitionSpec as P

TILE = 128
FAN = 4
CAP = 2
NB = 10
LAG = 128
HALVES = (64, 64)
BF = jnp.bfloat16
F32 = jnp.float32
SMEM = pltpu.SMEM
VMEM_LIMIT = 16 << 20
FLOPS_A_MICRO = 1e7
HIST_ROWS = 16
NAME_ROWS = 16


def raised_cosine(count, lag):
    low = math.log(2.0)
    high = math.log(lag + 1.0)
    spacing = (high - low) / (count - 1)
    stretched = np.log(np.arange(1, lag + 1).astype(np.float64) + 1.0)
    centers = low + spacing * np.arange(count).astype(np.float64)
    phases = np.clip(
        (stretched[None, :] - centers[:, None]) * (math.pi / (2.0 * spacing)), -math.pi, math.pi
    )
    shapes = 0.5 * (1.0 + np.cos(phases))
    return (shapes / np.sum(shapes, axis=1, keepdims=True)).astype(np.float32).astype(BF)


def toeplitz():
    basis = raised_cosine(NB, LAG)
    lag = LAG + np.arange(LAG)[None, :] - np.arange(2 * LAG)[:, None]
    inside = (lag >= 1) & (lag <= LAG)
    blocks = np.where(inside[None], basis[:, np.clip(lag - 1, 0, LAG - 1)], np.zeros((), BF))
    return np.ascontiguousarray(blocks.transpose(1, 0, 2).reshape(2 * LAG, NB * LAG))


def contract(a, b, dims):
    return lax.dot_general(a, b, ((dims[:1], dims[1:]), ((), ())), preferred_element_type=F32)


def find_slots(target, slots, lowest, highest, tiles_dev):
    for o in range(lowest.shape[0]):
        lowest[o] = tiles_dev
        highest[o] = -1
    for s in range(tiles_dev):
        for f in range(FAN):
            o = lax.div(target[f, s], tiles_dev)
            tile = lax.rem(target[f, s], tiles_dev)
            lowest[o] = jnp.minimum(lowest[o], tile)
            highest[o] = jnp.maximum(highest[o], tile)
    for s in range(tiles_dev):
        for f in range(FAN):
            o = lax.div(target[f, s], tiles_dev)
            tile = lax.rem(target[f, s], tiles_dev)
            slots[s * FAN + f] = o * CAP + (tile != lowest[o]).astype(jnp.int32)


def mixing_filter(mix, toep, filt):
    total = jnp.zeros((2 * LAG, LAG), F32)
    for b in range(NB):
        total += mix[b] * toep[:, b * LAG : (b + 1) * LAG].astype(F32)
    high = total.astype(BF)
    filt[:, :LAG] = high
    filt[:, LAG:] = (total - high.astype(F32)).astype(BF)


def mix_window(window, filt):
    both = jnp.dot(window, filt, preferred_element_type=F32)
    return (both[:, :LAG] + both[:, LAG:]).astype(BF)


def add_partials(slots, turned, mixed, total):
    total[...] = jnp.zeros_like(total)
    for s in range(turned.shape[0]):
        products = jnp.dot(turned[s], mixed[s], preferred_element_type=F32)
        for f in range(FAN):
            total[slots[s * FAN + f]] += products[f * TILE : (f + 1) * TILE]


def late_kernel(target_hbm, mix_hbm, spikes, weight, toep, *refs):
    x, mixed, filt, turned, slots = refs[:5]
    parts = refs[5:-9]
    target, mix, counts, weights, bases, total, lowest, highest, sems = refs[-9:]
    tiles_dev = x.shape[0]
    blocks = x.shape[2] // LAG
    pulls = [
        pltpu.make_async_copy(toep, bases, sems.at[0]),
        pltpu.make_async_copy(weight, weights, sems.at[1]),
        pltpu.make_async_copy(target_hbm, target, sems.at[2]),
        pltpu.make_async_copy(mix_hbm, mix, sems.at[3]),
    ]
    for k in range(blocks):
        at = pl.ds(k * LAG, LAG)
        pulls.append(pltpu.make_async_copy(spikes.at[at], counts.at[at], sems.at[4 + k]))
    for pull in pulls:
        pull.start()

    pulls[2].wait()
    find_slots(target, slots, lowest, highest, tiles_dev)
    pulls[3].wait()
    pulls[0].wait()
    mixing_filter(mix, bases, filt)
    before = None
    for k in range(blocks):
        pulls[4 + k].wait()
        now = counts[k * LAG : (k + 1) * LAG].astype(F32).T.astype(BF)
        x[:, :, k * LAG : (k + 1) * LAG] = now.reshape(tiles_dev, TILE, LAG)
        if k:
            got = mix_window(jnp.concatenate([before, now], axis=1), filt[...])
            mixed[:, :, (k - 1) * LAG : k * LAG] = got.reshape(tiles_dev, TILE, LAG)
        before = now

    pulls[1].wait()
    for s in range(tiles_dev):
        for f in range(FAN):
            turned[s, f * TILE : (f + 1) * TILE] = weights[s, f].astype(F32).T.astype(BF)
    add_partials(slots, turned, mixed, total)

    row = lax.broadcasted_iota(jnp.int32, (NAME_ROWS, LAG), 0)
    me = lax.axis_index("unit")
    for j, part in enumerate(parts):
        o = jnp.bitwise_xor(me, j)
        for k in range(1, blocks):
            for q in range(CAP):
                at = (k * CAP + q) * TILE
                block = total[o * CAP + q, :, (k - 1) * LAG : k * LAG]
                part[at : at + TILE] = block.astype(BF)
        high = highest[o]
        low = jnp.where(high < 0, -1, lowest[o])
        names = jnp.where(row == 0, low, jnp.where(row == 1, high, 0))
        part[blocks * CAP * TILE :] = names.astype(F32).astype(BF)


def early_kernel(slots, halo, x, filt, turned, *refs):
    kept = len(refs) // 2 - 1
    mixed_out, outs, total = refs[kept], refs[kept + 1 : -1], refs[-1]
    units = x.shape[0] * TILE
    now = halo[...].astype(F32).T.astype(BF)
    window = jnp.concatenate([now, x[...].reshape(units, LAG)], axis=1)
    mixed_out[...] = mix_window(window, filt[...]).reshape(mixed_out.shape)
    add_partials(slots, turned, mixed_out, total)
    me = lax.axis_index("unit")
    for k, out in enumerate(outs):
        for q in range(CAP):
            block = total[jnp.bitwise_xor(me, k) * CAP + q]
            out[q * TILE : (q + 1) * TILE] = block.astype(BF)


def windows(extended, count):
    return jnp.concatenate([extended[:, k * LAG : (k + 2) * LAG] for k in range(count)], axis=0)


def logit_kernel(x, halo, toep, hist_weight, bias, stim_filter, stimulus, out, history, rows):
    rows[...] = jnp.zeros_like(rows)
    rows[:NB] = hist_weight[...]
    rows[NB : NB + 1] = bias[...]
    blocks = x.shape[2] // LAG

    def one(s, _):
        units = pl.ds(pl.multiple_of(s * TILE, TILE), TILE)
        columns = rows[:, units].T
        start = contract(stim_filter[:, units], stimulus[...], (0, 0)) + columns[:, NB : NB + 1]
        total = [start[:, k * LAG : (k + 1) * LAG] for k in range(blocks)]
        before = halo[:, units].astype(F32).T.astype(BF)
        window = windows(jnp.concatenate([before, x[s]], axis=1), blocks)
        for c in range(0, NB, 2):
            both = jnp.dot(window, toep[:, c * LAG : (c + 2) * LAG], preferred_element_type=F32)
            for b in (c, c + 1):
                weight = columns[:, b : b + 1]
                piece = both[:, (b - c) * LAG : (b - c + 1) * LAG]
                for k in range(blocks):
                    part = piece[k * TILE : (k + 1) * TILE]
                    history[s, b, :, k * LAG : (k + 1) * LAG] = part
                    total[k] += weight * part
        for k in range(blocks):
            out[s, :, k * LAG : (k + 1) * LAG] = total[k]
        return 0

    lax.fori_loop(0, x.shape[0], one, 0)


def resid_kernel(parts, logit, x, *refs):
    total, rounded, ids = refs[-3:]
    refs = refs[:-3]
    count = (len(refs) - 1) // (1 + len(parts))
    got, resid, sends = refs[:count], refs[count], refs[count + 1 :]
    blocks = x.shape[2] // LAG
    for j in range(count):
        names = got[j][blocks * CAP * TILE :].astype(F32)
        for q in range(CAP):
            ids[j * CAP + q] = jnp.max(names[q : q + 1]).astype(jnp.int32)
    total[...] = logit[...]
    for j in range(count):
        for q in range(CAP):
            tile = ids[j * CAP + q]

            @pl.when(tile >= 0)
            def _():
                for k in range(blocks):
                    at = (k * CAP + q) * TILE
                    total[tile, :, k * LAG : (k + 1) * LAG] += got[j][at : at + TILE].astype(F32)

    for j in range(logit.shape[0]):
        r = x[j].astype(F32) - jnp.exp(total[j])
        resid[j] = r
        rounded[j] = r.astype(BF)
    for half, part in enumerate(parts):
        first = sum(parts[:half])
        for k in range(count):
            send = sends[half * count + k]
            for q in range(CAP):
                tile = ids[k * CAP + q]

                @pl.when(tile >= 0)
                def _():
                    send[q] = rounded[tile, first : first + part]

                @pl.when(tile < 0)
                def _():
                    send[q] = jnp.zeros(send.shape[1:], BF)


def peer(shift, count):
    return lax.rem(lax.axis_index("tm") + shift, count)


def own_kernel(history, stimulus, residuals, *refs):
    outs, (wide, stim, sums) = refs[:-3], refs[-3:]
    channels = stimulus.shape[0]
    rows = sums.shape[0]
    wide[...] = jnp.zeros_like(wide)
    wide[:channels] = stimulus[...]
    sums[...] = jnp.zeros_like(sums)
    lane = lax.broadcasted_iota(jnp.int32, (TILE, sums.shape[1]), 1)

    def folded(value):
        total = value[:, :LAG]
        for k in range(LAG, value.shape[1], LAG):
            total += value[:, k : k + LAG]
        return jnp.sum(total, axis=1, keepdims=True)

    def one(s, _):
        resid = residuals[s]
        units = pl.ds(pl.multiple_of(s * TILE, TILE), TILE)
        stim[units] = contract(resid.astype(BF), wide[...], (1, 1))
        columns = [folded(resid * history[s, b]) for b in range(NB)]
        column = folded(resid)
        high = column.astype(BF).astype(F32)
        first = channels + HIST_ROWS * lax.div(s * TILE, rows)
        block = jnp.zeros((TILE, sums.shape[1]), F32)
        for b, column in enumerate(columns + [high, column - high]):
            block = jnp.where(lane == first + b, column, block)
        at = pl.ds(pl.multiple_of(lax.rem(s * TILE, rows), TILE), TILE)
        sums[at] += block
        return 0

    lax.fori_loop(0, history.shape[0], one, 0)
    for shift, out in enumerate(outs):
        first = pl.multiple_of(peer(shift, len(outs)) * rows, TILE)
        out[...] = (stim[pl.ds(first, rows)] + sums[...]).astype(out.dtype)


def finish_kernel(scale, *refs):
    parts, (bias_out, hist_out, stim_out) = refs[:-3], refs[-3:]
    total = parts[0][...]
    for part in parts[1:]:
        total += part[:, part.shape[1] - total.shape[1] :].astype(F32)
    total *= scale
    channels, rows = stim_out.shape
    flat = total.T
    stim_out[...] = flat[:channels]
    for g in range(hist_out.shape[1] // rows):
        first = channels + HIST_ROWS * g
        at = slice(g * rows, (g + 1) * rows)
        hist_out[:, at] = flat[first : first + NB]
        bias_out[:, at] = flat[first + NB : first + NB + 1] + flat[first + NB + 1 : first + NB + 2]


def grad_kernel(count, extras, slots, mixed_early, mixed_late, *refs):
    recv, extra = refs[:count], refs[count : count + extras]
    outs, (table, chosen, grads) = refs[count + extras : -3], refs[-3:]
    part = recv[0].shape[1]
    rows = TILE // len(outs)
    me = lax.axis_index("unit")
    for k in range(count):
        table[pl.ds(jnp.bitwise_xor(me, k) * CAP, CAP)] = recv[k][...]
    for s in range(mixed_early.shape[0]):
        for f in range(FAN):
            chosen[s, f * part : (f + 1) * part] = table[slots[s * FAN + f]]
        mixed = jnp.concatenate([mixed_early[s], mixed_late[s]], axis=1)
        grads[s] = contract(mixed, chosen[s], (1, 1))
    for shift, out in enumerate(outs):
        first = pl.multiple_of(peer(shift, len(outs)) * rows, rows)
        block = grads[:, pl.ds(first, rows)].astype(out.dtype)
        out[:, : FAN * part] = block.reshape(out.shape[0], FAN * part)
        if extras and shift:
            out[:, FAN * part :] = extra[shift - 1][...]


def final_kernel(scale, parts_in, *refs):
    pieces_in, out = refs[:-1], refs[-1]
    halves = len(parts_in)
    count = len(pieces_in) // halves
    sums = []
    for half, part in enumerate(parts_in):
        wide = FAN * part
        mine = pieces_in[half * count : (half + 1) * count]
        total = mine[0][:, :wide].astype(F32)
        for piece in mine[1:]:
            total += piece[:, :wide].astype(F32)
        sums.append((total * scale).reshape(out.shape[0], out.shape[2], wide))
    for f in range(FAN):
        pieces = [
            total[:, :, f * part : (f + 1) * part]
            for total, part in zip(sums, parts_in, strict=True)
        ]
        out[:, f] = jnp.concatenate(pieces, axis=2)


def to_peers(pieces):
    count = len(pieces)
    got = [pieces[0]]
    for shift in range(1, count):
        pairs = [(i, (i + shift) % count) for i in range(count)]
        got.append(lax.ppermute(pieces[shift], "tm", pairs))
    return got


def to_units(pieces):
    got = [pieces[0]]
    for k in range(1, len(pieces)):
        got.append(lax.ppermute(pieces[k], "unit", [(i, i ^ k) for i in range(len(pieces))]))
    return got


def call(kernel, name, micros, **kw):
    limit = pltpu.CompilerParams(vmem_limit_bytes=VMEM_LIMIT)
    cost = pl.CostEstimate(
        flops=int(micros * FLOPS_A_MICRO), bytes_accessed=1 << 20, transcendentals=0
    )
    return pl.pallas_call(kernel, name=name, compiler_params=limit, cost_estimate=cost, **kw)


def vmem():
    return pl.BlockSpec(memory_space=pltpu.VMEM)


def smem():
    return pl.BlockSpec(memory_space=SMEM)


def whole(shape, at=None):
    spot = at or (0,) * len(shape)
    return pl.BlockSpec(shape, lambda *_: spot)


def per_tile(shape, axis=0):
    return pl.BlockSpec(shape, lambda s: tuple(s if a == axis else 0 for a in range(len(shape))))


def struct(shape, dtype):
    return jax.ShapeDtypeStruct(shape, dtype)


def far(array):
    return pltpu.with_memory_space_constraint(array, pltpu.HBM)


def shards(
    spikes, stimulus, bias, hist_weight, stim_filter, coupling_mix, coupling_target, coupling_weight
):
    time_dev, units_dev = spikes.shape
    tiles_dev = units_dev // TILE
    channels = stimulus.shape[1]
    unit_count = lax.axis_size("unit")
    time_count = lax.axis_size("tm")
    time_total = time_dev * time_count
    slots = unit_count * CAP
    late = time_dev - LAG
    toep = jnp.asarray(toeplitz())

    tail = spikes[time_dev - LAG :].astype(BF)
    halo = lax.ppermute(tail, "tm", [(i, i + 1) for i in range(time_count - 1)])

    hbm = pl.BlockSpec(memory_space=pltpu.HBM)
    entry = [coupling_target.T, coupling_mix, spikes, coupling_weight, toep]
    message = struct((CAP * time_dev + NAME_ROWS, LAG), BF)
    x, mixed_late, filt, turned, slot_table, *parts = call(
        late_kernel,
        "late",
        5,
        in_specs=[hbm] * len(entry),
        out_specs=[vmem()] * 4 + [smem()] + [vmem()] * unit_count,
        out_shape=[
            struct((tiles_dev, TILE, time_dev), BF),
            struct((tiles_dev, TILE, late), BF),
            struct((2 * LAG, 2 * LAG), BF),
            struct((tiles_dev, FAN * TILE, TILE), BF),
            struct((tiles_dev * FAN,), jnp.int32),
        ]
        + [message] * unit_count,
        scratch_shapes=[
            SMEM((FAN, tiles_dev), jnp.int32),
            SMEM(coupling_mix.shape, F32),
            pltpu.VMEM((time_dev, units_dev), jnp.int32),
            pltpu.VMEM((tiles_dev, FAN, TILE, TILE), BF),
            pltpu.VMEM((2 * LAG, NB * LAG), BF),
            pltpu.VMEM((slots, TILE, late), F32),
            SMEM((unit_count,), jnp.int32),
            SMEM((unit_count,), jnp.int32),
            pltpu.SemaphoreType.DMA((4 + time_dev // LAG,)),
        ],
    )(*[far(a) for a in entry])
    block_whole = whole((tiles_dev, TILE, LAG))
    anywhere = pl.BlockSpec(memory_space=pl.ANY)
    mixed_early, *parts = call(
        early_kernel,
        "early",
        2,
        grid=(1,),
        in_specs=[
            smem(),
            whole((LAG, units_dev)),
            block_whole,
            whole(filt.shape),
            whole(turned.shape),
        ]
        + [anywhere] * unit_count,
        out_specs=[block_whole] + [whole((CAP * TILE, LAG))] * unit_count,
        out_shape=[struct((tiles_dev, TILE, LAG), BF)] + [message] * unit_count,
        scratch_shapes=[pltpu.VMEM((slots, TILE, LAG), F32)],
        input_output_aliases={5 + k: 1 + k for k in range(unit_count)},
    )(slot_table, halo, x, filt, turned, *parts)
    got_parts = to_units(parts)
    stimulus_t = stimulus.T
    logit, history = call(
        logit_kernel,
        "logit",
        5,
        in_specs=[vmem()] * 7,
        out_shape=[
            struct((tiles_dev, TILE, time_dev), F32),
            pltpu.VMEM((tiles_dev, NB, TILE, time_dev), F32),
        ],
        scratch_shapes=[pltpu.VMEM((TILE, units_dev), F32)],
    )(x, halo, toep, hist_weight, bias.reshape(1, -1), stim_filter.T, stimulus_t)
    resid, *sends = call(
        functools.partial(resid_kernel, HALVES),
        "resid",
        2,
        in_specs=[vmem()] * (2 + unit_count),
        out_shape=[struct((tiles_dev, TILE, time_dev), F32)]
        + [struct((CAP, part, time_dev), BF) for part in HALVES for _ in range(unit_count)],
        scratch_shapes=[
            pltpu.VMEM((tiles_dev, TILE, time_dev), F32),
            pltpu.VMEM((tiles_dev, TILE, time_dev), BF),
            SMEM((slots,), jnp.int32),
        ],
    )(logit, x, *got_parts)
    sends = [sends[half * unit_count : (half + 1) * unit_count] for half in range(len(HALVES))]

    own_rows = units_dev // time_count
    wide = -(-(channels + HIST_ROWS * time_count) // TILE) * TILE
    own, *extra = call(
        own_kernel,
        "own",
        4,
        in_specs=[vmem()] * 3,
        out_shape=[
            struct((own_rows, wide), F32 if shift == 0 else BF) for shift in range(time_count)
        ],
        scratch_shapes=[
            pltpu.VMEM((wide, time_dev), BF),
            pltpu.VMEM((units_dev, wide), F32),
            pltpu.VMEM((own_rows, wide), F32),
        ],
    )(history, stimulus_t, resid)

    grads = []
    for send, part in zip(sends, HALVES, strict=True):
        got = to_units(send)
        extras = [] if grads else extra
        widths = [FAN * part] + [FAN * part + (wide if extras else 0)] * (time_count - 1)
        pieces = call(
            functools.partial(grad_kernel, unit_count, len(extras)),
            "grad",
            2,
            in_specs=[smem()] + [vmem()] * (2 + unit_count + len(extras)),
            out_shape=[struct((own_rows, width), BF) for width in widths],
            scratch_shapes=[
                pltpu.VMEM((slots, part, time_dev), BF),
                pltpu.VMEM((tiles_dev, FAN * part, time_dev), BF),
                pltpu.VMEM((tiles_dev, TILE, FAN * part), F32),
            ],
        )(slot_table, mixed_early, mixed_late, *got, *extras)
        grads += to_peers(pieces)
    grad_bias, grad_hist, grad_stim = call(
        functools.partial(finish_kernel, 1.0 / time_total),
        "finish",
        1,
        out_shape=[
            struct((1, units_dev), F32),
            struct((NB, units_dev), F32),
            struct((channels, own_rows), F32),
        ],
    )(own, *grads[1:time_count])
    grad_coupling = call(
        functools.partial(final_kernel, 1.0 / time_total, HALVES),
        "final",
        2,
        out_shape=struct((tiles_dev, FAN, TILE // time_count, TILE), F32),
    )(*grads)
    return (grad_bias.reshape(-1), grad_hist, grad_stim.T, grad_coupling)


def solution(mesh):
    return jax.shard_map(
        shards,
        mesh=mesh,
        in_specs=(
            P("tm", "unit"),
            P("tm", None),
            P("unit"),
            P(None, "unit"),
            P("unit", None),
            P(),
            P("unit", None),
            P("unit", None, None, None),
        ),
        out_specs=(
            P("unit"),
            P(None, "unit"),
            P(("unit", "tm"), None),
            P("unit", None, "tm", None),
        ),
        check_vma=False,
    )
```

```python
import functools
import math

import jax
import jax.numpy as jnp
import numpy as np
from jax import lax
from jax.experimental import pallas as pl
from jax.experimental.pallas import tpu as pltpu
from jax.sharding import PartitionSpec as P

TILE = 128
FAN = 4
CAP = 2
NB = 10
LAG = 128
HALVES = (64, 64)
BF = jnp.bfloat16
F32 = jnp.float32
SMEM = pltpu.SMEM
VMEM_LIMIT = 16 << 20
FLOPS_A_MICRO = 1e7
HIST_ROWS = 16
NAME_ROWS = 16


def raised_cosine(count, lag):
    low = math.log(2.0)
    high = math.log(lag + 1.0)
    spacing = (high - low) / (count - 1)
    stretched = np.log(np.arange(1, lag + 1).astype(np.float64) + 1.0)
    centers = low + spacing * np.arange(count).astype(np.float64)
    phases = np.clip(
        (stretched[None, :] - centers[:, None]) * (math.pi / (2.0 * spacing)), -math.pi, math.pi
    )
    shapes = 0.5 * (1.0 + np.cos(phases))
    return (shapes / np.sum(shapes, axis=1, keepdims=True)).astype(np.float32).astype(BF)


def toeplitz():
    basis = raised_cosine(NB, LAG)
    lag = LAG + np.arange(LAG)[None, :] - np.arange(2 * LAG)[:, None]
    inside = (lag >= 1) & (lag <= LAG)
    blocks = np.where(inside[None], basis[:, np.clip(lag - 1, 0, LAG - 1)], np.zeros((), BF))
    return np.ascontiguousarray(blocks.transpose(1, 0, 2).reshape(2 * LAG, NB * LAG))


def contract(a, b, dims):
    return lax.dot_general(a, b, ((dims[:1], dims[1:]), ((), ())), preferred_element_type=F32)


def find_slots(target, slots, lowest, highest, tiles_dev):
    for o in range(lowest.shape[0]):
        lowest[o] = tiles_dev
        highest[o] = -1
    for s in range(tiles_dev):
        for f in range(FAN):
            o = lax.div(target[f, s], tiles_dev)
            tile = lax.rem(target[f, s], tiles_dev)
            lowest[o] = jnp.minimum(lowest[o], tile)
            highest[o] = jnp.maximum(highest[o], tile)
    for s in range(tiles_dev):
        for f in range(FAN):
            o = lax.div(target[f, s], tiles_dev)
            tile = lax.rem(target[f, s], tiles_dev)
            slots[s * FAN + f] = o * CAP + (tile != lowest[o]).astype(jnp.int32)


def mixing_filter(mix, toep, filt):
    total = jnp.zeros((2 * LAG, LAG), F32)
    for b in range(NB):
        total += mix[b] * toep[:, b * LAG : (b + 1) * LAG].astype(F32)
    high = total.astype(BF)
    filt[:, :LAG] = high
    filt[:, LAG:] = (total - high.astype(F32)).astype(BF)


def mix_window(window, filt):
    both = jnp.dot(window, filt, preferred_element_type=F32)
    return (both[:, :LAG] + both[:, LAG:]).astype(BF)


def add_partials(slots, turned, mixed, total):
    total[...] = jnp.zeros_like(total)
    for s in range(turned.shape[0]):
        products = jnp.dot(turned[s], mixed[s], preferred_element_type=F32)
        for f in range(FAN):
            total[slots[s * FAN + f]] += products[f * TILE : (f + 1) * TILE]


def late_kernel(target_hbm, mix_hbm, spikes, weight, toep, *refs):
    x, mixed, filt, turned, slots = refs[:5]
    parts = refs[5:-9]
    target, mix, counts, weights, bases, total, lowest, highest, sems = refs[-9:]
    tiles_dev = x.shape[0]
    blocks = x.shape[2] // LAG
    pulls = [
        pltpu.make_async_copy(toep, bases, sems.at[0]),
        pltpu.make_async_copy(weight, weights, sems.at[1]),
        pltpu.make_async_copy(target_hbm, target, sems.at[2]),
        pltpu.make_async_copy(mix_hbm, mix, sems.at[3]),
    ]
    for k in range(blocks):
        at = pl.ds(k * LAG, LAG)
        pulls.append(pltpu.make_async_copy(spikes.at[at], counts.at[at], sems.at[4 + k]))
    for pull in pulls:
        pull.start()

    pulls[2].wait()
    find_slots(target, slots, lowest, highest, tiles_dev)
    pulls[3].wait()
    pulls[0].wait()
    mixing_filter(mix, bases, filt)
    before = None
    for k in range(blocks):
        pulls[4 + k].wait()
        now = counts[k * LAG : (k + 1) * LAG].astype(F32).T.astype(BF)
        x[:, :, k * LAG : (k + 1) * LAG] = now.reshape(tiles_dev, TILE, LAG)
        if k:
            got = mix_window(jnp.concatenate([before, now], axis=1), filt[...])
            mixed[:, :, (k - 1) * LAG : k * LAG] = got.reshape(tiles_dev, TILE, LAG)
        before = now

    pulls[1].wait()
    for s in range(tiles_dev):
        for f in range(FAN):
            turned[s, f * TILE : (f + 1) * TILE] = weights[s, f].astype(F32).T.astype(BF)
    add_partials(slots, turned, mixed, total)

    row = lax.broadcasted_iota(jnp.int32, (NAME_ROWS, LAG), 0)
    me = lax.axis_index("unit")
    for j, part in enumerate(parts):
        o = jnp.bitwise_xor(me, j)
        for k in range(1, blocks):
            for q in range(CAP):
                at = (k * CAP + q) * TILE
                block = total[o * CAP + q, :, (k - 1) * LAG : k * LAG]
                part[at : at + TILE] = block.astype(BF)
        high = highest[o]
        low = jnp.where(high < 0, -1, lowest[o])
        names = jnp.where(row == 0, low, jnp.where(row == 1, high, 0))
        part[blocks * CAP * TILE :] = names.astype(F32).astype(BF)


def early_kernel(slots, halo, x, filt, turned, *refs):
    kept = len(refs) // 2 - 1
    mixed_out, outs, total = refs[kept], refs[kept + 1 : -1], refs[-1]
    units = x.shape[0] * TILE
    now = halo[...].astype(F32).T.astype(BF)
    window = jnp.concatenate([now, x[...].reshape(units, LAG)], axis=1)
    mixed_out[...] = mix_window(window, filt[...]).reshape(mixed_out.shape)
    add_partials(slots, turned, mixed_out, total)
    me = lax.axis_index("unit")
    for k, out in enumerate(outs):
        for q in range(CAP):
            block = total[jnp.bitwise_xor(me, k) * CAP + q]
            out[q * TILE : (q + 1) * TILE] = block.astype(BF)


def windows(extended, count):
    return jnp.concatenate([extended[:, k * LAG : (k + 2) * LAG] for k in range(count)], axis=0)


def logit_kernel(x, halo, toep, hist_weight, bias, stim_filter, stimulus, out, history, rows):
    rows[...] = jnp.zeros_like(rows)
    rows[:NB] = hist_weight[...]
    rows[NB : NB + 1] = bias[...]
    blocks = x.shape[2] // LAG

    def one(s, _):
        units = pl.ds(pl.multiple_of(s * TILE, TILE), TILE)
        columns = rows[:, units].T
        start = contract(stim_filter[:, units], stimulus[...], (0, 0)) + columns[:, NB : NB + 1]
        total = [start[:, k * LAG : (k + 1) * LAG] for k in range(blocks)]
        before = halo[:, units].astype(F32).T.astype(BF)
        window = windows(jnp.concatenate([before, x[s]], axis=1), blocks)
        for c in range(0, NB, 2):
            both = jnp.dot(window, toep[:, c * LAG : (c + 2) * LAG], preferred_element_type=F32)
            for b in (c, c + 1):
                weight = columns[:, b : b + 1]
                piece = both[:, (b - c) * LAG : (b - c + 1) * LAG]
                for k in range(blocks):
                    part = piece[k * TILE : (k + 1) * TILE]
                    history[s, b, :, k * LAG : (k + 1) * LAG] = part
                    total[k] += weight * part
        for k in range(blocks):
            out[s, :, k * LAG : (k + 1) * LAG] = total[k]
        return 0

    lax.fori_loop(0, x.shape[0], one, 0)


def resid_kernel(parts, logit, x, *refs):
    total, rounded, ids = refs[-3:]
    refs = refs[:-3]
    count = (len(refs) - 1) // (1 + len(parts))
    got, resid, sends = refs[:count], refs[count], refs[count + 1 :]
    blocks = x.shape[2] // LAG
    for j in range(count):
        names = got[j][blocks * CAP * TILE :].astype(F32)
        for q in range(CAP):
            ids[j * CAP + q] = jnp.max(names[q : q + 1]).astype(jnp.int32)
    total[...] = logit[...]
    for j in range(count):
        for q in range(CAP):
            tile = ids[j * CAP + q]

            @pl.when(tile >= 0)
            def _():
                for k in range(blocks):
                    at = (k * CAP + q) * TILE
                    total[tile, :, k * LAG : (k + 1) * LAG] += got[j][at : at + TILE].astype(F32)

    for j in range(logit.shape[0]):
        r = x[j].astype(F32) - jnp.exp(total[j])
        resid[j] = r
        rounded[j] = r.astype(BF)
    for half, part in enumerate(parts):
        first = sum(parts[:half])
        for k in range(count):
            send = sends[half * count + k]
            for q in range(CAP):
                tile = ids[k * CAP + q]

                @pl.when(tile >= 0)
                def _():
                    send[q] = rounded[tile, first : first + part]

                @pl.when(tile < 0)
                def _():
                    send[q] = jnp.zeros(send.shape[1:], BF)


def peer(shift, count):
    return lax.rem(lax.axis_index("tm") + shift, count)


def own_kernel(history, stimulus, residuals, *refs):
    outs, (wide, stim, sums) = refs[:-3], refs[-3:]
    channels = stimulus.shape[0]
    rows = sums.shape[0]
    wide[...] = jnp.zeros_like(wide)
    wide[:channels] = stimulus[...]
    sums[...] = jnp.zeros_like(sums)
    lane = lax.broadcasted_iota(jnp.int32, (TILE, sums.shape[1]), 1)

    def folded(value):
        total = value[:, :LAG]
        for k in range(LAG, value.shape[1], LAG):
            total += value[:, k : k + LAG]
        return jnp.sum(total, axis=1, keepdims=True)

    def one(s, _):
        resid = residuals[s]
        units = pl.ds(pl.multiple_of(s * TILE, TILE), TILE)
        stim[units] = contract(resid.astype(BF), wide[...], (1, 1))
        columns = [folded(resid * history[s, b]) for b in range(NB)]
        column = folded(resid)
        high = column.astype(BF).astype(F32)
        first = channels + HIST_ROWS * lax.div(s * TILE, rows)
        block = jnp.zeros((TILE, sums.shape[1]), F32)
        for b, column in enumerate(columns + [high, column - high]):
            block = jnp.where(lane == first + b, column, block)
        at = pl.ds(pl.multiple_of(lax.rem(s * TILE, rows), TILE), TILE)
        sums[at] += block
        return 0

    lax.fori_loop(0, history.shape[0], one, 0)
    for shift, out in enumerate(outs):
        first = pl.multiple_of(peer(shift, len(outs)) * rows, TILE)
        out[...] = (stim[pl.ds(first, rows)] + sums[...]).astype(out.dtype)


def finish_kernel(scale, *refs):
    parts, (bias_out, hist_out, stim_out) = refs[:-3], refs[-3:]
    total = parts[0][...]
    for part in parts[1:]:
        total += part[:, part.shape[1] - total.shape[1] :].astype(F32)
    total *= scale
    channels, rows = stim_out.shape
    flat = total.T
    stim_out[...] = flat[:channels]
    for g in range(hist_out.shape[1] // rows):
        first = channels + HIST_ROWS * g
        at = slice(g * rows, (g + 1) * rows)
        hist_out[:, at] = flat[first : first + NB]
        bias_out[:, at] = flat[first + NB : first + NB + 1] + flat[first + NB + 1 : first + NB + 2]


def grad_kernel(count, extras, slots, mixed_early, mixed_late, *refs):
    recv, extra = refs[:count], refs[count : count + extras]
    outs, (table, chosen, grads) = refs[count + extras : -3], refs[-3:]
    part = recv[0].shape[1]
    rows = TILE // len(outs)
    me = lax.axis_index("unit")
    for k in range(count):
        table[pl.ds(jnp.bitwise_xor(me, k) * CAP, CAP)] = recv[k][...]
    for s in range(mixed_early.shape[0]):
        for f in range(FAN):
            chosen[s, f * part : (f + 1) * part] = table[slots[s * FAN + f]]
        mixed = jnp.concatenate([mixed_early[s], mixed_late[s]], axis=1)
        grads[s] = contract(mixed, chosen[s], (1, 1))
    for shift, out in enumerate(outs):
        first = pl.multiple_of(peer(shift, len(outs)) * rows, rows)
        block = grads[:, pl.ds(first, rows)].astype(out.dtype)
        out[:, : FAN * part] = block.reshape(out.shape[0], FAN * part)
        if extras and shift:
            out[:, FAN * part :] = extra[shift - 1][...]


def final_kernel(scale, parts_in, *refs):
    pieces_in, out = refs[:-1], refs[-1]
    halves = len(parts_in)
    count = len(pieces_in) // halves
    sums = []
    for half, part in enumerate(parts_in):
        wide = FAN * part
        mine = pieces_in[half * count : (half + 1) * count]
        total = mine[0][:, :wide].astype(F32)
        for piece in mine[1:]:
            total += piece[:, :wide].astype(F32)
        sums.append((total * scale).reshape(out.shape[0], out.shape[2], wide))
    for f in range(FAN):
        pieces = [
            total[:, :, f * part : (f + 1) * part]
            for total, part in zip(sums, parts_in, strict=True)
        ]
        out[:, f] = jnp.concatenate(pieces, axis=2)


def to_peers(pieces):
    count = len(pieces)
    got = [pieces[0]]
    for shift in [1, *range(count - 1, 1, -1)]:
        pairs = [(i, (i + shift) % count) for i in range(count)]
        got.append(lax.ppermute(pieces[shift], "tm", pairs))
    return got


def to_units(pieces):
    got = [pieces[0]]
    for k in range(1, len(pieces)):
        got.append(lax.ppermute(pieces[k], "unit", [(i, i ^ k) for i in range(len(pieces))]))
    return got


def call(kernel, name, micros, **kw):
    limit = pltpu.CompilerParams(vmem_limit_bytes=VMEM_LIMIT)
    cost = pl.CostEstimate(
        flops=int(micros * FLOPS_A_MICRO), bytes_accessed=1 << 20, transcendentals=0
    )
    return pl.pallas_call(kernel, name=name, compiler_params=limit, cost_estimate=cost, **kw)


def vmem():
    return pl.BlockSpec(memory_space=pltpu.VMEM)


def smem():
    return pl.BlockSpec(memory_space=SMEM)


def whole(shape, at=None):
    spot = at or (0,) * len(shape)
    return pl.BlockSpec(shape, lambda *_: spot)


def per_tile(shape, axis=0):
    return pl.BlockSpec(shape, lambda s: tuple(s if a == axis else 0 for a in range(len(shape))))


def struct(shape, dtype):
    return jax.ShapeDtypeStruct(shape, dtype)


def far(array):
    return pltpu.with_memory_space_constraint(array, pltpu.HBM)


def shards(
    spikes, stimulus, bias, hist_weight, stim_filter, coupling_mix, coupling_target, coupling_weight
):
    time_dev, units_dev = spikes.shape
    tiles_dev = units_dev // TILE
    channels = stimulus.shape[1]
    unit_count = lax.axis_size("unit")
    time_count = lax.axis_size("tm")
    time_total = time_dev * time_count
    slots = unit_count * CAP
    late = time_dev - LAG
    toep = jnp.asarray(toeplitz())

    tail = spikes[time_dev - LAG :].astype(BF)
    halo = lax.ppermute(tail, "tm", [(i, i + 1) for i in range(time_count - 1)])

    hbm = pl.BlockSpec(memory_space=pltpu.HBM)
    entry = [coupling_target.T, coupling_mix, spikes, coupling_weight, toep]
    message = struct((CAP * time_dev + NAME_ROWS, LAG), BF)
    x, mixed_late, filt, turned, slot_table, *parts = call(
        late_kernel,
        "late",
        5,
        in_specs=[hbm] * len(entry),
        out_specs=[vmem()] * 4 + [smem()] + [vmem()] * unit_count,
        out_shape=[
            struct((tiles_dev, TILE, time_dev), BF),
            struct((tiles_dev, TILE, late), BF),
            struct((2 * LAG, 2 * LAG), BF),
            struct((tiles_dev, FAN * TILE, TILE), BF),
            struct((tiles_dev * FAN,), jnp.int32),
        ]
        + [message] * unit_count,
        scratch_shapes=[
            SMEM((FAN, tiles_dev), jnp.int32),
            SMEM(coupling_mix.shape, F32),
            pltpu.VMEM((time_dev, units_dev), jnp.int32),
            pltpu.VMEM((tiles_dev, FAN, TILE, TILE), BF),
            pltpu.VMEM((2 * LAG, NB * LAG), BF),
            pltpu.VMEM((slots, TILE, late), F32),
            SMEM((unit_count,), jnp.int32),
            SMEM((unit_count,), jnp.int32),
            pltpu.SemaphoreType.DMA((4 + time_dev // LAG,)),
        ],
    )(*[far(a) for a in entry])
    block_whole = whole((tiles_dev, TILE, LAG))
    anywhere = pl.BlockSpec(memory_space=pl.ANY)
    mixed_early, *parts = call(
        early_kernel,
        "early",
        2,
        grid=(1,),
        in_specs=[
            smem(),
            whole((LAG, units_dev)),
            block_whole,
            whole(filt.shape),
            whole(turned.shape),
        ]
        + [anywhere] * unit_count,
        out_specs=[block_whole] + [whole((CAP * TILE, LAG))] * unit_count,
        out_shape=[struct((tiles_dev, TILE, LAG), BF)] + [message] * unit_count,
        scratch_shapes=[pltpu.VMEM((slots, TILE, LAG), F32)],
        input_output_aliases={5 + k: 1 + k for k in range(unit_count)},
    )(slot_table, halo, x, filt, turned, *parts)
    got_parts = to_units(parts)
    stimulus_t = stimulus.T
    logit, history = call(
        logit_kernel,
        "logit",
        5,
        in_specs=[vmem()] * 7,
        out_shape=[
            struct((tiles_dev, TILE, time_dev), F32),
            pltpu.VMEM((tiles_dev, NB, TILE, time_dev), F32),
        ],
        scratch_shapes=[pltpu.VMEM((TILE, units_dev), F32)],
    )(x, halo, toep, hist_weight, bias.reshape(1, -1), stim_filter.T, stimulus_t)
    resid, *sends = call(
        functools.partial(resid_kernel, HALVES),
        "resid",
        2,
        in_specs=[vmem()] * (2 + unit_count),
        out_shape=[struct((tiles_dev, TILE, time_dev), F32)]
        + [struct((CAP, part, time_dev), BF) for part in HALVES for _ in range(unit_count)],
        scratch_shapes=[
            pltpu.VMEM((tiles_dev, TILE, time_dev), F32),
            pltpu.VMEM((tiles_dev, TILE, time_dev), BF),
            SMEM((slots,), jnp.int32),
        ],
    )(logit, x, *got_parts)
    sends = [sends[half * unit_count : (half + 1) * unit_count] for half in range(len(HALVES))]

    own_rows = units_dev // time_count
    wide = -(-(channels + HIST_ROWS * time_count) // TILE) * TILE
    own, *extra = call(
        own_kernel,
        "own",
        4,
        in_specs=[vmem()] * 3,
        out_shape=[
            struct((own_rows, wide), F32 if shift == 0 else BF) for shift in range(time_count)
        ],
        scratch_shapes=[
            pltpu.VMEM((wide, time_dev), BF),
            pltpu.VMEM((units_dev, wide), F32),
            pltpu.VMEM((own_rows, wide), F32),
        ],
    )(history, stimulus_t, resid)

    grads = []
    for send, part in zip(sends, HALVES, strict=True):
        got = to_units(send)
        extras = [] if grads else extra
        widths = [FAN * part] + [FAN * part + (wide if extras else 0)] * (time_count - 1)
        pieces = call(
            functools.partial(grad_kernel, unit_count, len(extras)),
            "grad",
            2,
            in_specs=[smem()] + [vmem()] * (2 + unit_count + len(extras)),
            out_shape=[struct((own_rows, width), BF) for width in widths],
            scratch_shapes=[
                pltpu.VMEM((slots, part, time_dev), BF),
                pltpu.VMEM((tiles_dev, FAN * part, time_dev), BF),
                pltpu.VMEM((tiles_dev, TILE, FAN * part), F32),
            ],
        )(slot_table, mixed_early, mixed_late, *got, *extras)
        grads += to_peers(pieces)
    grad_bias, grad_hist, grad_stim = call(
        functools.partial(finish_kernel, 1.0 / time_total),
        "finish",
        1,
        out_shape=[
            struct((1, units_dev), F32),
            struct((NB, units_dev), F32),
            struct((channels, own_rows), F32),
        ],
    )(own, *grads[1:time_count])
    grad_coupling = call(
        functools.partial(final_kernel, 1.0 / time_total, HALVES),
        "final",
        2,
        out_shape=struct((tiles_dev, FAN, TILE // time_count, TILE), F32),
    )(*grads)
    return (grad_bias.reshape(-1), grad_hist, grad_stim.T, grad_coupling)


def solution(mesh):
    return jax.shard_map(
        shards,
        mesh=mesh,
        in_specs=(
            P("tm", "unit"),
            P("tm", None),
            P("unit"),
            P(None, "unit"),
            P("unit", None),
            P(),
            P("unit", None),
            P("unit", None, None, None),
        ),
        out_specs=(
            P("unit"),
            P(None, "unit"),
            P(("unit", "tm"), None),
            P("unit", None, "tm", None),
        ),
        check_vma=False,
    )
```
